256 devices in a mesh: wide: 32 (over x, z_hi, core), narrow: 8 (over z_lo, y).
Axes of the slice: x: 4, y: 4, z: 8 (z_hi: 4, z_lo: 2; z = z_hi * 2 + z_lo), core: 2. Of those that a mesh axis runs over, the one named last changes fastest.
Arguments:
- state_slab: float32 [256, 262144], P(('wide', 'narrow')), may hold values from -6 to 6
- angles: float32 [2, 26], replicated, may hold values from -3.140625 to 3.140625
- qubit_order: int32 [26], replicated, may hold values from 0 to 25, each once
- entangler_pairs: int32 [2, 26, 2], replicated, may hold values from 0 to 25, all different within a row
Outputs:
- final_state: float32 [256, 262144], P(('wide', 'narrow'))
The draws below stay inside these ranges and needn't reach their ends.
Inputs may be any that keep to these rules, and one draw needn't show every extreme that they name: `qubit_order`: every qubit number appears exactly once. `entangler_pairs`: the two qubits of each row differ.
All inputs are finite; a program needn't handle non-finite values.
Results may differ from the reference program's by a relative error of at most 0.00013.
Values sent between devices are 32-bit elements; how exact they have to be, the bound alone decides.
No kernel may reach another device: no remote copies, remote signals or barrier semaphores. Data moves between devices by JAX's collectives and lax.ppermute only.
A program may use at most 64 MiB of HBM per device.

```python
import jax
import jax.numpy as jnp
from jax import lax

LOCAL = 262144
QUBITS = 26
HIGH = 256
LAYERS = 2


def block_scale(rng, extent, cuts, least, largest):
    def one(position, parts):
        draws = jax.random.uniform(jax.random.fold_in(jax.random.fold_in(rng, 6), position), (parts,), jnp.float32, least / len(cuts), largest / len(cuts))
        return jnp.repeat(jnp.exp(draws), extent[position] // parts).reshape((-1,) + (1,) * (len(extent) - position - 1))

    level = one(*cuts[0])
    for cut in cuts[1:]:
        level = level * one(*cut)
    return level


def choose_distinct(own_key, rows, number_of, top, lift):
    ranking = jax.random.permutation(jax.random.fold_in(own_key, 1), number_of)
    favour = ranking
    for power in range(3):
        favour = favour * favour // number_of
    favour = favour * lift // number_of
    chance = jax.random.randint(jax.random.fold_in(own_key, 2), (rows, number_of), 0, 4096) + favour
    sure = jax.random.permutation(jax.random.fold_in(own_key, 3), rows)[jnp.arange(number_of) % rows]
    chance = jnp.where(jnp.arange(rows)[:, None] == sure[None, :], 1 << 14, chance)
    priority = chance * number_of + jnp.arange(number_of)
    return lax.top_k(priority.astype(jnp.int32), top)[1].astype(jnp.int32)


def gaussian(stream_key, extent, width, limit, pieces=(), kind=jnp.bfloat16):
    array = width * jax.random.normal(stream_key, extent, jnp.float32)
    if pieces:
        array = array * block_scale(stream_key, extent, pieces, -0.22, 0.18)
    return jnp.clip(array, -limit, limit).astype(kind)


def setup_inputs(seed: int = 0) -> dict:
    key_list = jax.random.split(jax.random.key(seed), 5)
    return {
        "state_slab": gaussian(key_list[0], (HIGH, LOCAL), 1.0, 6.0, ((0, 256),), jnp.float32),
        "angles": jnp.clip(jax.random.uniform(key_list[1], (LAYERS, QUBITS), jnp.float32, -3.140625, 3.140625), -3.140625, 3.140625),
        "qubit_order": jax.random.permutation(key_list[2], QUBITS).astype(jnp.int32),
        "entangler_pairs": choose_distinct(key_list[3], LAYERS * QUBITS, QUBITS, 2, 0).reshape((LAYERS, QUBITS, 2)),
    }


PRECISE = lax.Precision.HIGHEST


def rotations(angle_values):
    half_angle = 0.5 * angle_values
    cosine = jnp.cos(half_angle)
    sine_part = jnp.sin(half_angle)
    top_entries = jnp.stack([cosine, -sine_part], axis=-1)
    bottom_entries = jnp.stack([sine_part, cosine], axis=-1)
    return jnp.stack([top_entries, bottom_entries], axis=-2)


def block_matrix(rotation_set, qubit_list):
    matrix = rotation_set[qubit_list[0]]
    for qubit_index in qubit_list[1:]:
        matrix = jnp.kron(rotation_set[qubit_index], matrix)
    return matrix


def apply_bits(amplitudes, matrix, first_bit, bit_count, total_bits):
    outer_size = 2 ** (total_bits - first_bit - bit_count)
    inner_size = 2 ** first_bit
    block_size = 2 ** bit_count
    if inner_size == 1:
        shaped = amplitudes.reshape(outer_size, block_size)
        result = jnp.dot(shaped, matrix.T, precision=PRECISE)
    elif outer_size == 1:
        shaped = amplitudes.reshape(block_size, inner_size)
        result = jnp.dot(matrix, shaped, precision=PRECISE)
    else:
        shaped = amplitudes.reshape(outer_size, block_size, inner_size)
        result = jnp.einsum("ij,xjb->xib", matrix, shaped, precision=PRECISE)
    return result.reshape(-1)


def entangle(amplitudes, pair_rows, total_bits):
    low_count = total_bits // 2
    high_count = total_bits - low_count
    qubit_ids = jnp.arange(total_bits, dtype=jnp.int32)
    low_index = jnp.arange(2 ** low_count, dtype=jnp.int32)
    high_index = jnp.arange(2 ** high_count, dtype=jnp.int32)
    low_shift = jnp.minimum(qubit_ids, low_count - 1)
    high_shift = jnp.maximum(qubit_ids - low_count, 0)
    low_table = jnp.where(qubit_ids[None, :] < low_count, (low_index[:, None] >> low_shift[None, :]) & 1, 0).astype(jnp.float32)
    high_table = jnp.where(qubit_ids[None, :] >= low_count, (high_index[:, None] >> high_shift[None, :]) & 1, 0).astype(jnp.float32)
    first_hot = (pair_rows[:, 0][:, None] == qubit_ids[None, :]).astype(jnp.float32)
    second_hot = (pair_rows[:, 1][:, None] == qubit_ids[None, :]).astype(jnp.float32)
    couple = jnp.dot(first_hot.T, second_hot, precision=PRECISE)
    symmetric = couple + couple.T
    high_self = jnp.sum(jnp.dot(high_table, couple, precision=PRECISE) * high_table, axis=1)
    low_self = jnp.sum(jnp.dot(low_table, couple, precision=PRECISE) * low_table, axis=1)
    cross_left = jnp.dot(high_table, symmetric, precision=PRECISE)
    cross = jnp.dot(cross_left, low_table.T, precision=PRECISE)
    parity = high_self[:, None] + low_self[None, :] + cross
    signs = 1.0 - 2.0 * jnp.mod(parity, 2.0)
    return (amplitudes.reshape(2 ** high_count, 2 ** low_count) * signs).reshape(-1)


def reference(state_slab, angles, qubit_order, entangler_pairs):
    total_bits = QUBITS
    amplitudes = state_slab.reshape(-1)
    for layer_number in range(LAYERS):
        rotation_set = rotations(jnp.take(angles[layer_number], qubit_order, axis=0))
        first_bit = 0
        while first_bit < total_bits:
            bit_count = min(7, total_bits - first_bit)
            matrix = block_matrix(rotation_set, list(range(first_bit, first_bit + bit_count)))
            amplitudes = apply_bits(amplitudes, matrix, first_bit, bit_count, total_bits)
            first_bit = first_bit + bit_count
        amplitudes = entangle(amplitudes, entangler_pairs[layer_number], total_bits)
    return amplitudes.reshape(state_slab.shape)
```

```python
import functools

import jax
import jax.numpy as jnp
from jax import lax
from jax.experimental import pallas as pl
from jax.experimental.pallas import tpu as pltpu
from jax.sharding import PartitionSpec as P

AXES = ("wide", "narrow")
ROWS = 2048
BLOCK = 256
BLOCKS = ROWS // BLOCK
SLICE = 32
VIRTUAL = 26
ABSENT = 27


def trig_table(angles, order, layer):
    lane = lax.broadcasted_iota(jnp.int32, (8, 128), 1)
    theta = jnp.zeros((8, 128), jnp.float32)
    for qubit in range(order.shape[0]):
        theta = jnp.where(lane == qubit, angles[layer, order[qubit]], theta)
    half = 0.5 * theta
    return jnp.cos(half), jnp.sin(half)


def entry(table, qubit):
    return table[0:1, qubit : qubit + 1]


def kron_matrix(trig, qubits, transpose=False):
    cosines, sines = trig
    size = 2 ** len(qubits)
    row = lax.broadcasted_iota(jnp.int32, (size, size), 0)
    column = lax.broadcasted_iota(jnp.int32, (size, size), 1)
    if transpose:
        row, column = column, row
    matrix = None
    for bit, qubit in enumerate(qubits):
        change = (row >> bit & 1) - (column >> bit & 1)
        if qubit is None:
            factor = jnp.where(change == 0, 1.0, 0.0)
        else:
            cosine = jnp.broadcast_to(entry(cosines, qubit), (size, size))
            sine = jnp.broadcast_to(entry(sines, qubit), (size, size))
            factor = jnp.where(change == 0, cosine, jnp.where(change > 0, sine, -sine))
        matrix = factor if matrix is None else matrix * factor
    return matrix


def block_matrix(trig, qubits):
    small = kron_matrix(trig, qubits[:7])
    cosine, sine = entry(trig[0], qubits[7]), entry(trig[1], qubits[7])
    same, up = small * cosine, small * sine
    return jnp.concatenate(
        [jnp.concatenate([same, -up], axis=1), jnp.concatenate([up, same], axis=1)], axis=0
    )


def split(values):
    high = values.astype(jnp.bfloat16)
    low = (values - high.astype(jnp.float32)).astype(jnp.bfloat16)
    return high, low


def product(left, right):
    dot = functools.partial(jnp.dot, preferred_element_type=jnp.float32)
    return dot(left[0], right[0]) + (dot(left[0], right[1]) + dot(left[1], right[0]))


def butterflies(parts, trig, qubits):
    for bit, qubit in enumerate(qubits):
        cosine, sine = entry(trig[0], qubit), entry(trig[1], qubit)
        out = list(parts)
        for low in range(len(parts)):
            if low >> bit & 1 == 0:
                high = low | 1 << bit
                out[low] = cosine * parts[low] - sine * parts[high]
                out[high] = sine * parts[low] + cosine * parts[high]
        parts = out
    return parts


def lane_indices(pairs, layer, groups):
    lane = lax.broadcasted_iota(jnp.int32, (8, 128), 1)
    result = jnp.full((8, 128), ABSENT, jnp.int32)
    for group, member in enumerate(groups):
        if member is None:
            result = jnp.where(lane >> 5 == group, VIRTUAL, result)
            continue
        for number in range(pairs.shape[1]):
            result = jnp.where(lane == 32 * group + number, pairs[layer, number, member], result)
    return result[0:1]


def features(index, first, second):
    index = index | 1 << VIRTUAL
    return ((index >> first) & (index >> second) & 1).astype(jnp.float32).astype(jnp.bfloat16)


def store_parities(parity, pairs, layer, device_shift, row_shift):
    device = lax.axis_index(AXES[0]) * lax.axis_size(AXES[1]) + lax.axis_index(AXES[1])
    row_first = lane_indices(pairs, layer, (0, 1, 0, None))
    row_second = lane_indices(pairs, layer, (0, 1, 1, None))
    lane_first = lane_indices(pairs, layer, (1, 0, None, 0))
    lane_second = lane_indices(pairs, layer, (1, 0, None, 1))
    column = lax.broadcasted_iota(jnp.int32, (128, 128), 0)
    right = features(column, lane_first, lane_second)
    for block in range(BLOCKS):
        row = lax.broadcasted_iota(jnp.int32, (BLOCK, 128), 0) + BLOCK * block
        index = (row >> 3 << row_shift) | ((row & 7) << 7) | device << device_shift
        left = features(index, row_first, row_second)
        parity[pl.ds(BLOCK * block, BLOCK), :] = lax.dot_general(
            left, right, (((1,), (1,)), ((), ())), preferred_element_type=jnp.float32
        )


def signed(values, parity):
    return jnp.where(parity.astype(jnp.int32) & 1 == 0, values, -values)


def first_kernel(angles, order, state, out, scratch):
    trig = trig_table(angles, order, 0)
    lanes = split(kron_matrix(trig, range(7), transpose=True))
    matrix = split(block_matrix(trig, range(7, 15)))
    for block in range(BLOCKS):
        rows = pl.ds(BLOCK * block, BLOCK)
        scratch[rows, :] = product(matrix, split(product(split(state[rows, :]), lanes)))
    for start in range(0, BLOCK, SLICE):
        places = [pl.ds(BLOCK * block + start, SLICE) for block in range(BLOCKS)]
        parts = butterflies([scratch[place, :] for place in places], trig, range(15, 18))
        for place, part in zip(places, parts):
            out[place, :] = part


def second_kernel(angles, order, pairs, state, out, scratch, parity):
    store_parities(parity, pairs, 0, 10, 18)
    first = trig_table(angles, order, 0)
    second = trig_table(angles, order, 1)
    identity = [None] * 3
    matrix = split(block_matrix(first, identity + list(range(18, 23))))
    for block in range(BLOCKS):
        rows = pl.ds(BLOCK * block, BLOCK)
        scratch[rows, :] = product(matrix, split(state[rows, :]))
    for start in range(0, BLOCK, SLICE):
        places = [pl.ds(BLOCK * block + start, SLICE) for block in range(BLOCKS)]
        parts = butterflies([scratch[place, :] for place in places], first, range(23, 26))
        parts = [signed(part, parity[place, :]) for part, place in zip(parts, places)]
        parts = butterflies(parts, second, range(23, 26))
        for place, part in zip(places, parts):
            scratch[place, :] = part
    matrix = split(block_matrix(second, identity + list(range(18, 23))))
    for block in range(BLOCKS):
        rows = pl.ds(BLOCK * block, BLOCK)
        out[rows, :] = product(matrix, split(scratch[rows, :]))


def third_kernel(angles, order, pairs, state, out, scratch, parity):
    store_parities(parity, pairs, 1, 18, 10)
    trig = trig_table(angles, order, 1)
    lanes = split(kron_matrix(trig, range(7), transpose=True))
    matrix = split(block_matrix(trig, range(7, 15)))
    for block in range(BLOCKS):
        rows = pl.ds(BLOCK * block, BLOCK)
        scratch[rows, :] = product(matrix, split(product(split(state[rows, :]), lanes)))
    for start in range(0, BLOCK, SLICE):
        places = [pl.ds(BLOCK * block + start, SLICE) for block in range(BLOCKS)]
        parts = butterflies([scratch[place, :] for place in places], trig, range(15, 18))
        for place, part in zip(places, parts):
            out[place, :] = signed(part, parity[place, :])


def call(kernel, scalars, state, scratches):
    return pl.pallas_call(
        kernel,
        out_shape=jax.ShapeDtypeStruct((ROWS, 128), jnp.float32),
        in_specs=[pl.BlockSpec(memory_space=pltpu.SMEM)] * len(scalars)
        + [pl.BlockSpec(memory_space=pltpu.VMEM)],
        out_specs=pl.BlockSpec(memory_space=pltpu.VMEM),
        scratch_shapes=[pltpu.VMEM((ROWS, 128), jnp.float32)] * scratches,
        compiler_params=pltpu.CompilerParams(vmem_limit_bytes=16 * 2**20),
    )(*scalars, state)


def exchange(state):
    chunks = state.reshape(256, 8, 128)
    return lax.all_to_all(chunks, AXES, 0, 0, tiled=True).reshape(ROWS, 128)


def local(state_slab, angles, qubit_order, entangler_pairs):
    state = state_slab.reshape(ROWS, 128)
    state = call(first_kernel, (angles, qubit_order), state, 1)
    state = exchange(state)
    state = call(second_kernel, (angles, qubit_order, entangler_pairs), state, 2)
    state = exchange(state)
    state = call(third_kernel, (angles, qubit_order, entangler_pairs), state, 2)
    return state.reshape(state_slab.shape)


def solution(mesh):
    in_specs = (P(AXES, None), P(), P(), P())
    return jax.shard_map(local, mesh=mesh, in_specs=in_specs, out_specs=P(AXES, None), check_vma=False)
```

```python
import functools

import jax
import jax.numpy as jnp
from jax import lax
from jax.experimental import pallas as pl
from jax.experimental.pallas import tpu as pltpu
from jax.sharding import PartitionSpec as P

AXES = ("wide", "narrow")
ROWS = 2048
BLOCK = 256
BLOCKS = ROWS // BLOCK
SLICE = 32
VIRTUAL = 26
ABSENT = 27


def trig_table(angles, order, layer):
    lane = lax.broadcasted_iota(jnp.int32, (8, 128), 1)
    theta = jnp.zeros((8, 128), jnp.float32)
    for qubit in range(order.shape[0]):
        theta = jnp.where(lane == qubit, angles[layer, order[qubit]], theta)
    half = 0.5 * theta
    return jnp.cos(half), jnp.sin(half)


def entry(table, qubit):
    return table[0:1, qubit : qubit + 1]


def kron_matrix(trig, qubits, transpose=False):
    cosines, sines = trig
    size = 2 ** len(qubits)
    row = lax.broadcasted_iota(jnp.int32, (size, size), 0)
    column = lax.broadcasted_iota(jnp.int32, (size, size), 1)
    if transpose:
        row, column = column, row
    matrix = None
    for bit, qubit in enumerate(qubits):
        change = (row >> bit & 1) - (column >> bit & 1)
        cosine = jnp.broadcast_to(entry(cosines, qubit), (size, size))
        sine = jnp.broadcast_to(entry(sines, qubit), (size, size))
        factor = jnp.where(change == 0, cosine, jnp.where(change > 0, sine, -sine))
        matrix = factor if matrix is None else matrix * factor
    return matrix


def split(values):
    high = values.astype(jnp.bfloat16)
    low = (values - high.astype(jnp.float32)).astype(jnp.bfloat16)
    return high, low


def row_matrix(trig, qubits):
    small = kron_matrix(trig, qubits[:7])
    cosine, sine = entry(trig[0], qubits[7]), entry(trig[1], qubits[7])
    same, up = small * cosine, small * sine
    matrix = jnp.concatenate(
        [jnp.concatenate([same, -up], axis=1), jnp.concatenate([up, same], axis=1)], axis=0
    )
    high, low = split(matrix)
    return jnp.concatenate([high, low, high], axis=1)


def stacked(left, right):
    left_high, left_low = split(left)
    right_high, right_low = split(right)
    high = jnp.concatenate([left_high, right_high], axis=1)
    low = jnp.concatenate([left_low, right_low], axis=1)
    return jnp.concatenate([high, high, low], axis=0)


def on_rows(matrix, left, right):
    both = jnp.dot(matrix, stacked(left, right), preferred_element_type=jnp.float32)
    return both[:, :128], both[:, 128:]


def lane_matrix(trig, qubits):
    high, low = split(kron_matrix(trig, qubits, transpose=True))
    return jnp.concatenate(
        [jnp.concatenate([high, low], axis=1), jnp.concatenate([high, jnp.zeros_like(low)], axis=1)],
        axis=0,
    )


def on_lanes(values, matrix):
    parts = jnp.concatenate(split(values), axis=1)
    both = jnp.dot(parts, matrix, preferred_element_type=jnp.float32)
    return both[:, :128] + both[:, 128:]


def butterflies(parts, trig, qubits):
    for bit, qubit in enumerate(qubits):
        cosine, sine = entry(trig[0], qubit), entry(trig[1], qubit)
        out = list(parts)
        for low in range(len(parts)):
            if low >> bit & 1 == 0:
                high = low | 1 << bit
                out[low] = cosine * parts[low] - sine * parts[high]
                out[high] = sine * parts[low] + cosine * parts[high]
        parts = out
    return parts


def lane_indices(pairs, layer, groups):
    lane = lax.broadcasted_iota(jnp.int32, (8, 128), 1)
    result = jnp.full((8, 128), ABSENT, jnp.int32)
    for group, member in enumerate(groups):
        if member is None:
            result = jnp.where(lane >> 5 == group, VIRTUAL, result)
            continue
        for number in range(pairs.shape[1]):
            result = jnp.where(lane == 32 * group + number, pairs[layer, number, member], result)
    return result[0:1]


def features(index, first, second):
    index = index | 1 << VIRTUAL
    return ((index >> first) & (index >> second) & 1).astype(jnp.float32).astype(jnp.bfloat16)


def store_signs(signs, pairs, layer, index_of):
    row_first = lane_indices(pairs, layer, (0, 1, 0, None))
    row_second = lane_indices(pairs, layer, (0, 1, 1, None))
    lane_first = lane_indices(pairs, layer, (1, 0, None, 0))
    lane_second = lane_indices(pairs, layer, (1, 0, None, 1))
    column = lax.broadcasted_iota(jnp.int32, (128, 128), 0)
    right = features(column, lane_first, lane_second)
    for block in range(BLOCKS):
        row = lax.broadcasted_iota(jnp.int32, (BLOCK, 128), 0)
        left = features(index_of(block, row), row_first, row_second)
        parity = lax.dot_general(
            left, right, (((1,), (1,)), ((), ())), preferred_element_type=jnp.float32
        )
        signs[pl.ds(BLOCK * block, BLOCK), :] = jnp.where(parity.astype(jnp.int32) & 1 == 0, 1.0, -1.0)


def tables_kernel(angles, order, pairs, middle_signs, last_signs, middle, last, lanes, trig_out):
    device = lax.axis_index(AXES[0]) * lax.axis_size(AXES[1]) + lax.axis_index(AXES[1])
    first = trig_table(angles, order, 0)
    second = trig_table(angles, order, 1)
    middle[0] = row_matrix(first, range(18, 26))
    middle[1] = row_matrix(second, range(18, 26))
    last[...] = row_matrix(second, range(7, 15))
    lanes[...] = lane_matrix(second, range(7))
    trig_out[0], trig_out[1] = second
    store_signs(middle_signs, pairs, 0, lambda block, row: row << 18 | device << 10 | block << 7)
    store_signs(last_signs, pairs, 1, lambda block, row: row + BLOCK * block << 7 | device << 18)


def first_kernel(angles, order, state, out, held, scratch, arrived):
    copies = []
    for pair in range(BLOCKS // 2):
        rows = pl.ds(2 * BLOCK * pair, 2 * BLOCK)
        copies.append(pltpu.make_async_copy(state.at[rows], held.at[rows], arrived.at[pair]))
        copies[-1].start()
    trig = trig_table(angles, order, 0)
    lanes = lane_matrix(trig, range(7))
    matrix = row_matrix(trig, range(7, 15))
    for pair in range(BLOCKS // 2):
        copies[pair].wait()
        here, there = (pl.ds(BLOCK * (2 * pair + side), BLOCK) for side in range(2))
        scratch[here, :], scratch[there, :] = on_rows(
            matrix, on_lanes(held[here, :], lanes), on_lanes(held[there, :], lanes)
        )
    for start in range(0, BLOCK, SLICE):
        places = [pl.ds(BLOCK * block + start, SLICE) for block in range(BLOCKS)]
        parts = butterflies([scratch[place, :] for place in places], trig, range(15, 18))
        for place, part in zip(places, parts):
            out[place, :] = part


def second_kernel(signs, matrices, state, out):
    for pair in range(4):
        here, there = (pl.ds(2 * pair + side, BLOCK, stride=8) for side in range(2))
        left, right = on_rows(matrices[0], state[here, :], state[there, :])
        left = left * signs[pl.ds(BLOCK * 2 * pair, BLOCK), :]
        right = right * signs[pl.ds(BLOCK * (2 * pair + 1), BLOCK), :]
        out[here, :], out[there, :] = on_rows(matrices[1], left, right)


def third_kernel(signs, matrix, lanes, trig, state, out, scratch, ready, sent):
    trig = trig[0], trig[1]
    for start in range(0, BLOCK, SLICE):
        places = [pl.ds(BLOCK * block + start, SLICE) for block in range(BLOCKS)]
        parts = butterflies([state[place, :] for place in places], trig, range(15, 18))
        for place, part in zip(places, parts):
            scratch[place, :] = part
    copies = []
    for pair in range(BLOCKS // 2):
        here, there = (pl.ds(BLOCK * (2 * pair + side), BLOCK) for side in range(2))
        left, right = on_rows(
            matrix[...], on_lanes(scratch[here, :], lanes[...]), on_lanes(scratch[there, :], lanes[...])
        )
        ready[here, :] = left * signs[here, :]
        ready[there, :] = right * signs[there, :]
        rows = pl.ds(2 * BLOCK * pair, 2 * BLOCK)
        copies.append(pltpu.make_async_copy(ready.at[rows], out.at[rows], sent.at[pair]))
        copies[-1].start()
    for copy in copies:
        copy.wait()


STATE = jax.ShapeDtypeStruct((ROWS, 128), jnp.float32)
HELD = pltpu.VMEM((ROWS, 128), jnp.float32)
PARAMS = pltpu.CompilerParams(vmem_limit_bytes=20 * 2**20)
VMEM, SMEM, HBM = (pl.BlockSpec(memory_space=space) for space in (pltpu.VMEM, pltpu.SMEM, pltpu.HBM))


def make_tables(angles, order, pairs):
    return pl.pallas_call(
        tables_kernel,
        out_shape=(
            STATE,
            STATE,
            jax.ShapeDtypeStruct((2, 256, 768), jnp.bfloat16),
            jax.ShapeDtypeStruct((256, 768), jnp.bfloat16),
            jax.ShapeDtypeStruct((256, 256), jnp.bfloat16),
            jax.ShapeDtypeStruct((2, 8, 128), jnp.float32),
        ),
        in_specs=[SMEM] * 3,
        out_specs=(VMEM,) * 6,
        compiler_params=PARAMS,
    )(angles, order, pairs)


def first(angles, order, state):
    return pl.pallas_call(
        first_kernel,
        out_shape=STATE,
        in_specs=[SMEM, SMEM, HBM],
        out_specs=VMEM,
        scratch_shapes=[HELD, HELD, pltpu.SemaphoreType.DMA((BLOCKS // 2,))],
        compiler_params=PARAMS,
    )(angles, order, state)


def second(signs, matrices, state):
    return pl.pallas_call(
        second_kernel, out_shape=STATE, in_specs=[VMEM] * 3, out_specs=VMEM, compiler_params=PARAMS
    )(signs, matrices, state)


def third(signs, matrix, lanes, trig, state):
    return pl.pallas_call(
        third_kernel,
        out_shape=STATE,
        in_specs=[VMEM] * 5,
        out_specs=HBM,
        scratch_shapes=[HELD, HELD, pltpu.SemaphoreType.DMA((BLOCKS // 2,))],
        compiler_params=PARAMS,
    )(signs, matrix, lanes, trig, state)


def exchange(state):
    chunks = state.reshape(256, 8, 128)
    return lax.all_to_all(chunks, AXES, 0, 0, tiled=True).reshape(ROWS, 128)


def local(state_slab, angles, qubit_order, entangler_pairs):
    middle_signs, last_signs, middle, last, lanes, trig = make_tables(angles, qubit_order, entangler_pairs)
    state = first(angles, qubit_order, state_slab.reshape(ROWS, 128))
    state = exchange(state)
    state = second(middle_signs, middle, state)
    state = exchange(state)
    state = third(last_signs, last, lanes, trig, state)
    return state.reshape(state_slab.shape)


def solution(mesh):
    in_specs = (P(AXES, None), P(), P(), P())
    return jax.shard_map(local, mesh=mesh, in_specs=in_specs, out_specs=P(AXES, None), check_vma=False)
```

```python
import functools

import jax
import jax.numpy as jnp
from jax import lax
from jax.experimental import pallas as pl
from jax.experimental.pallas import tpu as pltpu
from jax.sharding import Mesh
from jax.sharding import PartitionSpec as P

AXES = ("x", "z_hi", "core", "z_lo", "y")
SIZES = (4, 4, 2, 2, 4)
PEERS = ("y", "x", "z_hi", "z_lo", "core")
HIGH = (21, 20, 22, 23, 24, 25, 18, 19)
ROWS = 2048
BLOCK = 256
BLOCKS = ROWS // BLOCK
SLICE = 32
VIRTUAL = 26
ABSENT = 27


def trig_table(angles, order, layer):
    lane = lax.broadcasted_iota(jnp.int32, (8, 128), 1)
    theta = jnp.zeros((8, 128), jnp.float32)
    for qubit in range(order.shape[0]):
        theta = jnp.where(lane == qubit, angles[layer, order[qubit]], theta)
    half = 0.5 * theta
    return jnp.cos(half), jnp.sin(half)


def entry(table, qubit):
    return table[0:1, qubit : qubit + 1]


def kron_matrix(trig, qubits, transpose=False):
    cosines, sines = trig
    size = 2 ** len(qubits)
    row = lax.broadcasted_iota(jnp.int32, (size, size), 0)
    column = lax.broadcasted_iota(jnp.int32, (size, size), 1)
    if transpose:
        row, column = column, row
    matrix = None
    for bit, qubit in enumerate(qubits):
        change = (row >> bit & 1) - (column >> bit & 1)
        cosine = jnp.broadcast_to(entry(cosines, qubit), (size, size))
        sine = jnp.broadcast_to(entry(sines, qubit), (size, size))
        factor = jnp.where(change == 0, cosine, jnp.where(change > 0, sine, -sine))
        matrix = factor if matrix is None else matrix * factor
    return matrix


def split(values):
    high = values.astype(jnp.bfloat16)
    low = (values - high.astype(jnp.float32)).astype(jnp.bfloat16)
    return high, low


def row_matrix(trig, qubits):
    small = kron_matrix(trig, qubits[:7])
    cosine, sine = entry(trig[0], qubits[7]), entry(trig[1], qubits[7])
    same, up = small * cosine, small * sine
    matrix = jnp.concatenate(
        [jnp.concatenate([same, -up], axis=1), jnp.concatenate([up, same], axis=1)], axis=0
    )
    high, low = split(matrix)
    return jnp.concatenate([high, low, high], axis=1)


def stacked(left, right):
    left_high, left_low = split(left)
    right_high, right_low = split(right)
    high = jnp.concatenate([left_high, right_high], axis=1)
    low = jnp.concatenate([left_low, right_low], axis=1)
    return jnp.concatenate([high, high, low], axis=0)


def on_rows(matrix, left, right):
    both = jnp.dot(matrix, stacked(left, right), preferred_element_type=jnp.float32)
    return both[:, :128], both[:, 128:]


def lane_matrix(trig, qubits):
    high, low = split(kron_matrix(trig, qubits, transpose=True))
    return jnp.concatenate(
        [jnp.concatenate([high, low], axis=1), jnp.concatenate([high, jnp.zeros_like(low)], axis=1)],
        axis=0,
    )


def on_lanes(values, matrix):
    parts = jnp.concatenate(split(values), axis=1)
    both = jnp.dot(parts, matrix, preferred_element_type=jnp.float32)
    return both[:, :128] + both[:, 128:]


def butterflies(parts, trig, qubits):
    for bit, qubit in enumerate(qubits):
        cosine, sine = entry(trig[0], qubit), entry(trig[1], qubit)
        out = list(parts)
        for low in range(len(parts)):
            if low >> bit & 1 == 0:
                high = low | 1 << bit
                out[low] = cosine * parts[low] - sine * parts[high]
                out[high] = sine * parts[low] + cosine * parts[high]
        parts = out
    return parts


def lane_indices(pairs, layer, groups):
    lane = lax.broadcasted_iota(jnp.int32, (8, 128), 1)
    result = jnp.full((8, 128), ABSENT, jnp.int32)
    for group, member in enumerate(groups):
        if member is None:
            result = jnp.where(lane >> 5 == group, VIRTUAL, result)
            continue
        for number in range(pairs.shape[1]):
            result = jnp.where(lane == 32 * group + number, pairs[layer, number, member], result)
    return result[0:1]


def features(index, first, second):
    index = index | 1 << VIRTUAL
    return ((index >> first) & (index >> second) & 1).astype(jnp.float32).astype(jnp.bfloat16)


def store_signs(signs, pairs, layer, index_of):
    row_first = lane_indices(pairs, layer, (0, 1, 0, None))
    row_second = lane_indices(pairs, layer, (0, 1, 1, None))
    lane_first = lane_indices(pairs, layer, (1, 0, None, 0))
    lane_second = lane_indices(pairs, layer, (1, 0, None, 1))
    column = lax.broadcasted_iota(jnp.int32, (128, 128), 0)
    right = features(column, lane_first, lane_second)
    for block in range(BLOCKS):
        row = lax.broadcasted_iota(jnp.int32, (BLOCK, 128), 0)
        left = features(index_of(block, row), row_first, row_second)
        parity = lax.dot_general(
            left, right, (((1,), (1,)), ((), ())), preferred_element_type=jnp.float32
        )
        signs[pl.ds(BLOCK * block, BLOCK), :] = jnp.where(parity.astype(jnp.int32) & 1 == 0, 1.0, -1.0)


def place(axes):
    index = 0
    for axis in axes:
        index = index * lax.axis_size(axis) + lax.axis_index(axis)
    return index


def high_bits(peer):
    index = jnp.zeros_like(peer)
    for bit, qubit in enumerate(HIGH):
        index = index | (peer >> bit & 1) << qubit
    return index


def tables_kernel(angles, order, pairs, middle_signs, last_signs, middle, last, lanes, trig_out):
    device = place(AXES)
    peer = place(PEERS)
    first = trig_table(angles, order, 0)
    second = trig_table(angles, order, 1)
    middle[0] = row_matrix(first, HIGH)
    middle[1] = row_matrix(second, HIGH)
    last[...] = row_matrix(second, range(7, 15))
    lanes[...] = lane_matrix(second, range(7))
    trig_out[0], trig_out[1] = second
    store_signs(middle_signs, pairs, 0, lambda block, row: high_bits(row) | peer << 10 | block << 7)
    store_signs(last_signs, pairs, 1, lambda block, row: row + BLOCK * block << 7 | device << 18)


def first_kernel(angles_in, order_in, state, out, angles, order, held, scratch, small, arrived):
    tables = [
        pltpu.make_async_copy(angles_in, angles, small.at[0]),
        pltpu.make_async_copy(order_in, order, small.at[1]),
    ]
    for copy in tables:
        copy.start()
    copies = []
    for pair in range(BLOCKS // 2):
        rows = pl.ds(2 * BLOCK * pair, 2 * BLOCK)
        copies.append(pltpu.make_async_copy(state.at[rows], held.at[rows], arrived.at[pair]))
        copies[-1].start()
    for copy in tables:
        copy.wait()
    trig = trig_table(angles, order, 0)
    lanes = lane_matrix(trig, range(7))
    matrix = row_matrix(trig, range(7, 15))
    for pair in range(BLOCKS // 2):
        copies[pair].wait()
        here, there = (pl.ds(BLOCK * (2 * pair + side), BLOCK) for side in range(2))
        scratch[here, :], scratch[there, :] = on_rows(
            matrix, on_lanes(held[here, :], lanes), on_lanes(held[there, :], lanes)
        )
    for start in range(0, BLOCK, SLICE):
        places = [pl.ds(BLOCK * block + start, SLICE) for block in range(BLOCKS)]
        parts = butterflies([scratch[place, :] for place in places], trig, range(15, 18))
        for place, part in zip(places, parts):
            out[place, :] = part


def second_kernel(signs, matrices, state, out):
    for pair in range(4):
        here, there = (pl.ds(2 * pair + side, BLOCK, stride=8) for side in range(2))
        left, right = on_rows(matrices[0], state[here, :], state[there, :])
        left = left * signs[pl.ds(BLOCK * 2 * pair, BLOCK), :]
        right = right * signs[pl.ds(BLOCK * (2 * pair + 1), BLOCK), :]
        out[here, :], out[there, :] = on_rows(matrices[1], left, right)


def third_kernel(signs, matrix, lanes, trig, state, out, scratch, ready, sent):
    trig = trig[0], trig[1]
    for start in range(0, BLOCK, SLICE):
        places = [pl.ds(BLOCK * block + start, SLICE) for block in range(BLOCKS)]
        parts = butterflies([state[place, :] for place in places], trig, range(15, 18))
        for place, part in zip(places, parts):
            scratch[place, :] = part
    copies = []
    for pair in range(BLOCKS // 2):
        here, there = (pl.ds(BLOCK * (2 * pair + side), BLOCK) for side in range(2))
        left, right = on_rows(
            matrix[...], on_lanes(scratch[here, :], lanes[...]), on_lanes(scratch[there, :], lanes[...])
        )
        ready[here, :] = left * signs[here, :]
        ready[there, :] = right * signs[there, :]
        rows = pl.ds(2 * BLOCK * pair, 2 * BLOCK)
        copies.append(pltpu.make_async_copy(ready.at[rows], out.at[rows], sent.at[pair]))
        copies[-1].start()
    for copy in copies:
        copy.wait()


STATE = jax.ShapeDtypeStruct((ROWS, 128), jnp.float32)
HELD = pltpu.VMEM((ROWS, 128), jnp.float32)
PARAMS = pltpu.CompilerParams(vmem_limit_bytes=20 * 2**20)
VMEM, SMEM, HBM = (pl.BlockSpec(memory_space=space) for space in (pltpu.VMEM, pltpu.SMEM, pltpu.HBM))


def make_tables(angles, order, pairs):
    return pl.pallas_call(
        tables_kernel,
        out_shape=(
            HELD,
            HELD,
            pltpu.VMEM((2, 256, 768), jnp.bfloat16),
            pltpu.VMEM((256, 768), jnp.bfloat16),
            pltpu.VMEM((256, 256), jnp.bfloat16),
            pltpu.VMEM((2, 8, 128), jnp.float32),
        ),
        in_specs=[SMEM] * 3,
        out_specs=(VMEM,) * 6,
        compiler_params=PARAMS,
    )(angles, order, pairs)


def first(angles, order, state):
    return pl.pallas_call(
        first_kernel,
        out_shape=HELD,
        in_specs=[HBM] * 3,
        out_specs=VMEM,
        scratch_shapes=[
            pltpu.SMEM(angles.shape, jnp.float32),
            pltpu.SMEM(order.shape, jnp.int32),
            HELD,
            HELD,
            pltpu.SemaphoreType.DMA((2,)),
            pltpu.SemaphoreType.DMA((BLOCKS // 2,)),
        ],
        compiler_params=PARAMS,
    )(*(pltpu.with_memory_space_constraint(array, pltpu.HBM) for array in (angles, order, state)))


def second(signs, matrices, state):
    return pl.pallas_call(
        second_kernel, out_shape=HELD, in_specs=[VMEM] * 3, out_specs=VMEM, compiler_params=PARAMS
    )(signs, matrices, state)


def third(signs, matrix, lanes, trig, state):
    return pl.pallas_call(
        third_kernel,
        out_shape=STATE,
        in_specs=[VMEM] * 5,
        out_specs=HBM,
        scratch_shapes=[HELD, HELD, pltpu.SemaphoreType.DMA((BLOCKS // 2,))],
        compiler_params=PARAMS,
    )(signs, matrix, lanes, trig, state)


def exchange(state):
    chunks = state.reshape(256, 8, 128)
    return lax.all_to_all(chunks, PEERS, 0, 0, tiled=True).reshape(ROWS, 128)


def local(state_slab, angles, qubit_order, entangler_pairs):
    middle_signs, last_signs, middle, last, lanes, trig = make_tables(angles, qubit_order, entangler_pairs)
    state = first(angles, qubit_order, state_slab.reshape(ROWS, 128))
    state = exchange(state)
    state = second(middle_signs, middle, state)
    state = exchange(state)
    state = third(last_signs, last, lanes, trig, state)
    return state.reshape(state_slab.shape)


def solution(mesh):
    in_specs = (P(AXES, None), P(), P(), P())
    mesh = Mesh(mesh.devices.reshape(SIZES), AXES)
    return jax.shard_map(local, mesh=mesh, in_specs=in_specs, out_specs=P(AXES, None), check_vma=False)
```

```python
import functools

import jax
import jax.numpy as jnp
from jax import lax
from jax.experimental import pallas as pl
from jax.experimental.pallas import tpu as pltpu
from jax.sharding import Mesh
from jax.sharding import PartitionSpec as P

AXES = ("x", "z_hi", "core", "z_lo", "y")
SIZES = (4, 4, 2, 2, 4)
PEERS = ("y", "x", "z_hi", "z_lo", "core")
HIGH = (21, 20, 22, 23, 24, 25, 18, 19)
ROWS = 2048
BLOCK = 256
BLOCKS = ROWS // BLOCK
SLICE = 32
PARTS = 2
VIRTUAL = 26
ABSENT = 27


def trig_table(angles, order, layer):
    lane = lax.broadcasted_iota(jnp.int32, (8, 128), 1)
    theta = jnp.zeros((8, 128), jnp.float32)
    for qubit in range(order.shape[0]):
        theta = jnp.where(lane == qubit, angles[layer, order[qubit]], theta)
    half = 0.5 * theta
    return jnp.cos(half), jnp.sin(half)


def entry(table, qubit):
    return table[0:1, qubit : qubit + 1]


def kron_matrix(trig, qubits, transpose=False):
    cosines, sines = trig
    size = 2 ** len(qubits)
    row = lax.broadcasted_iota(jnp.int32, (size, size), 0)
    column = lax.broadcasted_iota(jnp.int32, (size, size), 1)
    if transpose:
        row, column = column, row
    matrix = None
    for bit, qubit in enumerate(qubits):
        change = (row >> bit & 1) - (column >> bit & 1)
        cosine = jnp.broadcast_to(entry(cosines, qubit), (size, size))
        sine = jnp.broadcast_to(entry(sines, qubit), (size, size))
        factor = jnp.where(change == 0, cosine, jnp.where(change > 0, sine, -sine))
        matrix = factor if matrix is None else matrix * factor
    return matrix


def split(values):
    high = values.astype(jnp.bfloat16)
    low = (values - high.astype(jnp.float32)).astype(jnp.bfloat16)
    return high, low


def row_matrix(trig, qubits):
    small = kron_matrix(trig, qubits[:7])
    cosine, sine = entry(trig[0], qubits[7]), entry(trig[1], qubits[7])
    same, up = small * cosine, small * sine
    matrix = jnp.concatenate(
        [jnp.concatenate([same, -up], axis=1), jnp.concatenate([up, same], axis=1)], axis=0
    )
    return jnp.concatenate(split(matrix), axis=1)


def stacked(left, right):
    left_high, left_low = split(left)
    right_high, right_low = split(right)
    high = jnp.concatenate([left_high, right_high], axis=1)
    low = jnp.concatenate([left_low, right_low], axis=1)
    return jnp.concatenate([high, high, low], axis=0)


def on_rows(matrix, left, right):
    matrix = jnp.concatenate([matrix, matrix[:, :BLOCK]], axis=1)
    both = jnp.dot(matrix, stacked(left, right), preferred_element_type=jnp.float32)
    return both[:, :128], both[:, 128:]


def lane_matrix(trig, qubits):
    return jnp.concatenate(split(kron_matrix(trig, qubits, transpose=True)), axis=1)


def on_lanes(values, matrix):
    high = matrix[:, :128]
    matrix = jnp.concatenate(
        [matrix, jnp.concatenate([high, jnp.zeros_like(high)], axis=1)], axis=0
    )
    parts = jnp.concatenate(split(values), axis=1)
    both = jnp.dot(parts, matrix, preferred_element_type=jnp.float32)
    return both[:, :128] + both[:, 128:]


def butterflies(parts, trig, qubits):
    for bit, qubit in enumerate(qubits):
        cosine, sine = entry(trig[0], qubit), entry(trig[1], qubit)
        out = list(parts)
        for low in range(len(parts)):
            if low >> bit & 1 == 0:
                high = low | 1 << bit
                out[low] = cosine * parts[low] - sine * parts[high]
                out[high] = sine * parts[low] + cosine * parts[high]
        parts = out
    return parts


def lane_indices(pairs, layer, groups):
    lane = lax.broadcasted_iota(jnp.int32, (8, 128), 1)
    result = jnp.full((8, 128), ABSENT, jnp.int32)
    for group, member in enumerate(groups):
        if member is None:
            result = jnp.where(lane >> 5 == group, VIRTUAL, result)
            continue
        for number in range(pairs.shape[2]):
            result = jnp.where(lane == 32 * group + number, pairs[layer, member, number], result)
    return result[0:1]


def features(index, first, second):
    index = index | 1 << VIRTUAL
    return ((index >> first) & (index >> second) & 1).astype(jnp.float32).astype(jnp.bfloat16)


def minus_bits(pairs, layer, first_bit, index_of):
    row_first = lane_indices(pairs, layer, (0, 1, 0, None))
    row_second = lane_indices(pairs, layer, (0, 1, 1, None))
    lane_first = lane_indices(pairs, layer, (1, 0, None, 0))
    lane_second = lane_indices(pairs, layer, (1, 0, None, 1))
    column = lax.broadcasted_iota(jnp.int32, (128, 128), 0)
    right = features(column, lane_first, lane_second)
    row = lax.broadcasted_iota(jnp.int32, (BLOCK, 128), 0)
    bits = jnp.zeros((BLOCK, 128), jnp.int32)
    for block in range(BLOCKS):
        left = features(index_of(block, row), row_first, row_second)
        parity = lax.dot_general(
            left, right, (((1,), (1,)), ((), ())), preferred_element_type=jnp.float32
        )
        bits = bits | (parity.astype(jnp.int32) & 1) << first_bit + block
    return bits


def signed(values, minus, bit):
    return jnp.where(minus & 1 << bit == 0, values, -values)


def fetch(*ways, semaphores):
    copies = [pltpu.make_async_copy(*way, semaphores.at[number]) for number, way in enumerate(ways)]
    for copy in copies:
        copy.start()
    for copy in copies:
        copy.wait()


def place(axes):
    index = 0
    for axis in axes:
        index = index * lax.axis_size(axis) + lax.axis_index(axis)
    return index


def high_bits(peer):
    index = jnp.zeros_like(peer)
    for bit, qubit in enumerate(HIGH):
        index = index | (peer >> bit & 1) << qubit
    return index


def tables_kernel(
    angles_in, order_in, pairs_in, minus, middle, last, lanes, trig_out, angles, order, pairs, small
):
    fetch((angles_in, angles), (order_in, order), (pairs_in, pairs), semaphores=small)
    device = place(AXES)
    peer = place(PEERS)
    first = trig_table(angles, order, 0)
    second = trig_table(angles, order, 1)
    middle[0] = row_matrix(first, HIGH)
    middle[1] = row_matrix(second, HIGH)
    last[...] = row_matrix(second, range(7, 15))
    lanes[...] = lane_matrix(second, range(7))
    trig_out[0], trig_out[1] = second
    middle_bits = minus_bits(
        pairs, 0, 0, lambda block, row: high_bits(row) | peer << 10 | block << 7
    )
    last_bits = minus_bits(
        pairs, 1, BLOCKS, lambda block, row: row + BLOCK * block << 7 | device << 18
    )
    minus[...] = middle_bits | last_bits


def first_kernel(angles_in, order_in, state, out, angles, order, held, scratch, small, arrived):
    copies = []
    for pair in range(BLOCKS // 2):
        rows = pl.ds(2 * pair, 2)
        copies.append(pltpu.make_async_copy(state.at[rows], held.at[rows], arrived.at[pair]))
        copies[-1].start()
    fetch((angles_in, angles), (order_in, order), semaphores=small)
    trig = trig_table(angles, order, 0)
    lanes = lane_matrix(trig, range(7))
    matrix = row_matrix(trig, range(7, 15))
    for copy in copies:
        copy.wait()
    swing(held, scratch, trig)
    for here in range(0, BLOCKS, 2):
        out[here], out[here + 1] = rotated(scratch, here, matrix, lanes)


def swing(state, scratch, trig):
    for start in range(0, BLOCK, SLICE):
        rows = pl.ds(start, SLICE)
        parts = [state[block, rows, :] for block in range(BLOCKS)]
        for block, part in enumerate(butterflies(parts, trig, range(15, 18))):
            scratch[block, rows, :] = part


def rotated(state, here, matrix, lanes):
    return on_rows(matrix, on_lanes(state[here], lanes), on_lanes(state[here + 1], lanes))


def second_kernel(minus, matrices, state, out):
    for pair in range(4):
        here, there = (pl.ds(2 * pair + side, BLOCK, stride=8) for side in range(2))
        left, right = on_rows(matrices[0], state[here, :], state[there, :])
        left = signed(left, minus[...], 2 * pair)
        right = signed(right, minus[...], 2 * pair + 1)
        out[here, :], out[there, :] = on_rows(matrices[1], left, right)


def third_kernel(minus, matrix, lanes, trig, state, out, scratch, ready, sent):
    swing(state, scratch, (trig[0], trig[1]))
    copies = []
    for part in range(PARTS):
        size = BLOCKS // PARTS
        for here in range(size * part, size * (part + 1), 2):
            for block, values in enumerate(rotated(scratch, here, matrix[...], lanes[...]), here):
                ready[block] = signed(values, minus[...], BLOCKS + block)
        blocks = pl.ds(size * part, size)
        copies.append(pltpu.make_async_copy(ready.at[blocks], out.at[blocks], sent.at[part]))
        copies[-1].start()
    for copy in copies:
        copy.wait()


HELD = pltpu.VMEM((ROWS, 128), jnp.float32)
IN_BLOCKS = pltpu.VMEM((BLOCKS, BLOCK, 128), jnp.float32)
PARAMS = pltpu.CompilerParams(vmem_limit_bytes=12 * 2**20)
VMEM, SMEM, HBM = (pl.BlockSpec(memory_space=space) for space in (pltpu.VMEM, pltpu.SMEM, pltpu.HBM))


def in_hbm(array):
    return pltpu.with_memory_space_constraint(array, pltpu.HBM)


def make_tables(angles, order, pairs):
    return pl.pallas_call(
        tables_kernel,
        out_shape=(
            pltpu.VMEM((BLOCK, 128), jnp.int32),
            pltpu.VMEM((2, 256, 512), jnp.bfloat16),
            pltpu.VMEM((256, 512), jnp.bfloat16),
            pltpu.VMEM((128, 256), jnp.bfloat16),
            pltpu.VMEM((2, 8, 128), jnp.float32),
        ),
        in_specs=[HBM] * 3,
        out_specs=(VMEM,) * 5,
        scratch_shapes=[
            pltpu.SMEM(angles.shape, jnp.float32),
            pltpu.SMEM(order.shape, jnp.int32),
            pltpu.SMEM(pairs.shape, jnp.int32),
            pltpu.SemaphoreType.DMA((3,)),
        ],
        compiler_params=PARAMS,
    )(*(in_hbm(array) for array in (angles, order, pairs)))


def first(angles, order, state):
    state = state.reshape(IN_BLOCKS.shape)
    return pl.pallas_call(
        first_kernel,
        out_shape=IN_BLOCKS,
        in_specs=[HBM] * 3,
        out_specs=VMEM,
        scratch_shapes=[
            pltpu.SMEM(angles.shape, jnp.float32),
            pltpu.SMEM(order.shape, jnp.int32),
            IN_BLOCKS,
            IN_BLOCKS,
            pltpu.SemaphoreType.DMA((2,)),
            pltpu.SemaphoreType.DMA((BLOCKS // 2,)),
        ],
        compiler_params=PARAMS,
    )(*(in_hbm(array) for array in (angles, order, state))).reshape(ROWS, 128)


def second(minus, matrices, state):
    return pl.pallas_call(
        second_kernel, out_shape=HELD, in_specs=[VMEM] * 3, out_specs=VMEM, compiler_params=PARAMS
    )(minus, matrices, state)


def third(minus, matrix, lanes, trig, state):
    return pl.pallas_call(
        third_kernel,
        out_shape=jax.ShapeDtypeStruct(IN_BLOCKS.shape, jnp.float32),
        in_specs=[VMEM] * 5,
        out_specs=HBM,
        scratch_shapes=[IN_BLOCKS, IN_BLOCKS, pltpu.SemaphoreType.DMA((PARTS,))],
        compiler_params=PARAMS,
    )(minus, matrix, lanes, trig, state.reshape(IN_BLOCKS.shape))


def exchange(state):
    chunks = state.reshape(256, 8, 128)
    return lax.all_to_all(chunks, PEERS, 0, 0, tiled=True).reshape(ROWS, 128)


def local(state_slab, angles, qubit_order, entangler_pairs):
    minus, middle, last, lanes, trig = make_tables(
        angles, qubit_order, entangler_pairs.transpose(0, 2, 1)
    )
    state = first(angles, qubit_order, state_slab.reshape(ROWS, 128))
    state = exchange(state)
    state = second(minus, middle, state)
    state = exchange(state)
    state = third(minus, last, lanes, trig, state)
    return state.reshape(state_slab.shape)


def solution(mesh):
    in_specs = (P(AXES, None), P(), P(), P())
    mesh = Mesh(mesh.devices.reshape(SIZES), AXES)
    return jax.shard_map(local, mesh=mesh, in_specs=in_specs, out_specs=P(AXES, None), check_vma=False)
```

```python
import functools

import jax
import jax.numpy as jnp
from jax import lax
from jax.experimental import pallas as pl
from jax.experimental.pallas import tpu as pltpu
from jax.sharding import Mesh
from jax.sharding import PartitionSpec as P

AXES = ("x", "z_hi", "core", "z_lo", "y")
SIZES = (4, 4, 2, 2, 4)
PEERS = ("z_hi", "z_lo", "y", "x", "core")
HIGH = (21, 24, 25, 18, 19, 20, 22, 23)
ROWS = 2048
BLOCK = 256
BLOCKS = ROWS // BLOCK
SLICE = 32
PARTS = 2
VIRTUAL = 26
ABSENT = 27


def trig_table(angles, order, layer):
    lane = lax.broadcasted_iota(jnp.int32, (8, 128), 1)
    theta = jnp.zeros((8, 128), jnp.float32)
    for qubit in range(order.shape[0]):
        theta = jnp.where(lane == qubit, angles[layer, order[qubit]], theta)
    half = 0.5 * theta
    return jnp.cos(half), jnp.sin(half)


def entry(table, qubit):
    return table[0:1, qubit : qubit + 1]


def kron_matrix(trig, qubits, transpose=False):
    cosines, sines = trig
    size = 2 ** len(qubits)
    row = lax.broadcasted_iota(jnp.int32, (size, size), 0)
    column = lax.broadcasted_iota(jnp.int32, (size, size), 1)
    if transpose:
        row, column = column, row
    matrix = None
    for bit, qubit in enumerate(qubits):
        change = (row >> bit & 1) - (column >> bit & 1)
        cosine = jnp.broadcast_to(entry(cosines, qubit), (size, size))
        sine = jnp.broadcast_to(entry(sines, qubit), (size, size))
        factor = jnp.where(change == 0, cosine, jnp.where(change > 0, sine, -sine))
        matrix = factor if matrix is None else matrix * factor
    return matrix


def split(values):
    high = values.astype(jnp.bfloat16)
    low = (values - high.astype(jnp.float32)).astype(jnp.bfloat16)
    return high, low


def row_matrix(trig, qubits):
    small = kron_matrix(trig, qubits[:7])
    cosine, sine = entry(trig[0], qubits[7]), entry(trig[1], qubits[7])
    same, up = small * cosine, small * sine
    matrix = jnp.concatenate(
        [jnp.concatenate([same, -up], axis=1), jnp.concatenate([up, same], axis=1)], axis=0
    )
    return jnp.concatenate(split(matrix), axis=1)


def stacked(left, right):
    left_high, left_low = split(left)
    right_high, right_low = split(right)
    high = jnp.concatenate([left_high, right_high], axis=1)
    low = jnp.concatenate([left_low, right_low], axis=1)
    return jnp.concatenate([high, high, low], axis=0)


def on_rows(matrix, left, right):
    matrix = jnp.concatenate([matrix, matrix[:, :BLOCK]], axis=1)
    both = jnp.dot(matrix, stacked(left, right), preferred_element_type=jnp.float32)
    return both[:, :128], both[:, 128:]


def lane_matrix(trig, qubits):
    return jnp.concatenate(split(kron_matrix(trig, qubits, transpose=True)), axis=1)


def on_lanes(values, matrix):
    high = matrix[:, :128]
    matrix = jnp.concatenate(
        [matrix, jnp.concatenate([high, jnp.zeros_like(high)], axis=1)], axis=0
    )
    parts = jnp.concatenate(split(values), axis=1)
    both = jnp.dot(parts, matrix, preferred_element_type=jnp.float32)
    return both[:, :128] + both[:, 128:]


def butterflies(parts, trig, qubits):
    for bit, qubit in enumerate(qubits):
        cosine, sine = entry(trig[0], qubit), entry(trig[1], qubit)
        out = list(parts)
        for low in range(len(parts)):
            if low >> bit & 1 == 0:
                high = low | 1 << bit
                out[low] = cosine * parts[low] - sine * parts[high]
                out[high] = sine * parts[low] + cosine * parts[high]
        parts = out
    return parts


def lane_indices(pairs, layer, groups):
    lane = lax.broadcasted_iota(jnp.int32, (8, 128), 1)
    result = jnp.full((8, 128), ABSENT, jnp.int32)
    for group, member in enumerate(groups):
        if member is None:
            result = jnp.where(lane >> 5 == group, VIRTUAL, result)
            continue
        for number in range(pairs.shape[2]):
            result = jnp.where(lane == 32 * group + number, pairs[layer, member, number], result)
    return result[0:1]


def features(index, first, second):
    index = index | 1 << VIRTUAL
    return ((index >> first) & (index >> second) & 1).astype(jnp.float32).astype(jnp.bfloat16)


def minus_bits(pairs, layer, first_bit, index_of):
    row_first = lane_indices(pairs, layer, (0, 1, 0, None))
    row_second = lane_indices(pairs, layer, (0, 1, 1, None))
    lane_first = lane_indices(pairs, layer, (1, 0, None, 0))
    lane_second = lane_indices(pairs, layer, (1, 0, None, 1))
    column = lax.broadcasted_iota(jnp.int32, (128, 128), 0)
    right = features(column, lane_first, lane_second)
    row = lax.broadcasted_iota(jnp.int32, (BLOCK, 128), 0)
    bits = jnp.zeros((BLOCK, 128), jnp.int32)
    for block in range(BLOCKS):
        left = features(index_of(block, row), row_first, row_second)
        parity = lax.dot_general(
            left, right, (((1,), (1,)), ((), ())), preferred_element_type=jnp.float32
        )
        bits = bits | (parity.astype(jnp.int32) & 1) << first_bit + block
    return bits


def signed(values, minus, bit):
    return jnp.where(minus & 1 << bit == 0, values, -values)


def fetch(*ways, semaphores):
    copies = [pltpu.make_async_copy(*way, semaphores.at[number]) for number, way in enumerate(ways)]
    for copy in copies:
        copy.start()
    for copy in copies:
        copy.wait()


def place(axes):
    index = 0
    for axis in axes:
        index = index * lax.axis_size(axis) + lax.axis_index(axis)
    return index


def high_bits(peer):
    index = jnp.zeros_like(peer)
    for bit, qubit in enumerate(HIGH):
        index = index | (peer >> bit & 1) << qubit
    return index


def tables_kernel(
    angles_in, order_in, pairs_in, minus, middle, last, lanes, trig_out, angles, order, pairs, small
):
    fetch((angles_in, angles), (order_in, order), (pairs_in, pairs), semaphores=small)
    device = place(AXES)
    peer = place(PEERS)
    first = trig_table(angles, order, 0)
    second = trig_table(angles, order, 1)
    middle[0] = row_matrix(first, HIGH)
    middle[1] = row_matrix(second, HIGH)
    last[...] = row_matrix(second, range(7, 15))
    lanes[...] = lane_matrix(second, range(7))
    trig_out[0], trig_out[1] = second
    middle_bits = minus_bits(
        pairs, 0, 0, lambda block, row: high_bits(row) | peer << 10 | block << 7
    )
    last_bits = minus_bits(
        pairs, 1, BLOCKS, lambda block, row: row + BLOCK * block << 7 | device << 18
    )
    minus[...] = middle_bits | last_bits


def first_kernel(angles_in, order_in, state, out, angles, order, held, scratch, ready, small, arrived, sent):
    copies = []
    for pair in range(BLOCKS // 2):
        blocks = pl.ds(2 * pair, 2)
        copies.append(pltpu.make_async_copy(state.at[blocks], held.at[blocks], arrived.at[pair]))
        copies[-1].start()
    fetch((angles_in, angles), (order_in, order), semaphores=small)
    trig = trig_table(angles, order, 0)
    lanes = lane_matrix(trig, range(7))
    matrix = row_matrix(trig, range(7, 15))
    for copy in copies:
        copy.wait()
    rotate(held, trig, matrix, lanes, None, out, scratch, ready, sent)


def rotate(state, trig, matrix, lanes, minus, out, scratch, ready, sent):
    for start in range(0, BLOCK, SLICE):
        rows = pl.ds(start, SLICE)
        parts = [state[block, rows, :] for block in range(BLOCKS)]
        for block, part in enumerate(butterflies(parts, trig, range(15, 18))):
            scratch[block, rows, :] = part
    turned = [on_lanes(scratch[block], lanes) for block in range(BLOCKS)]
    copies = []
    size = BLOCKS // PARTS
    for part in range(PARTS):
        for here in range(size * part, size * (part + 1), 2):
            for block, values in enumerate(on_rows(matrix, turned[here], turned[here + 1]), here):
                ready[block] = values if minus is None else signed(values, minus, BLOCKS + block)
        blocks = pl.ds(size * part, size)
        copies.append(pltpu.make_async_copy(ready.at[blocks], out.at[blocks], sent.at[part]))
        copies[-1].start()
    for copy in copies:
        copy.wait()


def second_kernel(minus, matrices, state, out):
    places = [pl.ds(row, BLOCK, stride=8) for row in range(8)]
    turned = []
    for here in range(0, 8, 2):
        pair = on_rows(matrices[0], state[places[here], :], state[places[here + 1], :])
        turned += [signed(values, minus[...], row) for row, values in enumerate(pair, here)]
    for here in range(0, 8, 2):
        pair = on_rows(matrices[1], turned[here], turned[here + 1])
        out[places[here], :], out[places[here + 1], :] = pair


def third_kernel(minus, matrix, lanes, trig, state, out, scratch, ready, sent):
    trig = trig[0], trig[1]
    rotate(state, trig, matrix[...], lanes[...], minus[...], out, scratch, ready, sent)


HELD = pltpu.VMEM((ROWS, 128), jnp.float32)
IN_BLOCKS = pltpu.VMEM((BLOCKS, BLOCK, 128), jnp.float32)
PARAMS = pltpu.CompilerParams(vmem_limit_bytes=12 * 2**20)
VMEM, SMEM, HBM = (pl.BlockSpec(memory_space=space) for space in (pltpu.VMEM, pltpu.SMEM, pltpu.HBM))


def in_hbm(array):
    return pltpu.with_memory_space_constraint(array, pltpu.HBM)


def make_tables(angles, order, pairs):
    return pl.pallas_call(
        tables_kernel,
        out_shape=(
            pltpu.VMEM((BLOCK, 128), jnp.int32),
            pltpu.VMEM((2, 256, 512), jnp.bfloat16),
            pltpu.VMEM((256, 512), jnp.bfloat16),
            pltpu.VMEM((128, 256), jnp.bfloat16),
            pltpu.VMEM((2, 8, 128), jnp.float32),
        ),
        in_specs=[HBM] * 3,
        out_specs=(VMEM,) * 5,
        scratch_shapes=[
            pltpu.SMEM(angles.shape, jnp.float32),
            pltpu.SMEM(order.shape, jnp.int32),
            pltpu.SMEM(pairs.shape, jnp.int32),
            pltpu.SemaphoreType.DMA((3,)),
        ],
        compiler_params=PARAMS,
    )(*(in_hbm(array) for array in (angles, order, pairs)))


def first(angles, order, state):
    state = state.reshape(IN_BLOCKS.shape)
    return pl.pallas_call(
        first_kernel,
        out_shape=pltpu.HBM(IN_BLOCKS.shape, jnp.float32),
        in_specs=[HBM] * 3,
        out_specs=HBM,
        scratch_shapes=[
            pltpu.SMEM(angles.shape, jnp.float32),
            pltpu.SMEM(order.shape, jnp.int32),
            IN_BLOCKS,
            IN_BLOCKS,
            IN_BLOCKS,
            pltpu.SemaphoreType.DMA((2,)),
            pltpu.SemaphoreType.DMA((BLOCKS // 2,)),
            pltpu.SemaphoreType.DMA((PARTS,)),
        ],
        compiler_params=PARAMS,
    )(*(in_hbm(array) for array in (angles, order, state))).reshape(ROWS, 128)


def second(minus, matrices, state):
    return pl.pallas_call(
        second_kernel, out_shape=HELD, in_specs=[VMEM] * 3, out_specs=VMEM, compiler_params=PARAMS
    )(minus, matrices, state)


def third(minus, matrix, lanes, trig, state):
    return pl.pallas_call(
        third_kernel,
        out_shape=jax.ShapeDtypeStruct(IN_BLOCKS.shape, jnp.float32),
        in_specs=[VMEM] * 5,
        out_specs=HBM,
        scratch_shapes=[IN_BLOCKS, IN_BLOCKS, pltpu.SemaphoreType.DMA((PARTS,))],
        compiler_params=PARAMS,
    )(minus, matrix, lanes, trig, state.reshape(IN_BLOCKS.shape))


def exchange(state):
    chunks = state.reshape(256, 8, 128)
    return lax.all_to_all(chunks, PEERS, 0, 0, tiled=True).reshape(ROWS, 128)


def local(state_slab, angles, qubit_order, entangler_pairs):
    minus, middle, last, lanes, trig = make_tables(
        angles, qubit_order, entangler_pairs.transpose(0, 2, 1)
    )
    state = first(angles, qubit_order, state_slab.reshape(ROWS, 128))
    state = exchange(state)
    state = second(minus, middle, state)
    state = exchange(state)
    state = third(minus, last, lanes, trig, state)
    return state.reshape(state_slab.shape)


def solution(mesh):
    in_specs = (P(AXES, None), P(), P(), P())
    mesh = Mesh(mesh.devices.reshape(SIZES), AXES)
    return jax.shard_map(local, mesh=mesh, in_specs=in_specs, out_specs=P(AXES, None), check_vma=False)
```

```python
import functools

import jax
import jax.numpy as jnp
from jax import lax
from jax.experimental import pallas as pl
from jax.experimental.pallas import tpu as pltpu
from jax.sharding import Mesh
from jax.sharding import PartitionSpec as P

AXES = ("x", "z_hi", "core", "z_lo", "y")
SIZES = (4, 4, 2, 2, 4)
PEERS = ("z_hi", "z_lo", "y", "x", "core")
HIGH = (21, 24, 25, 18, 19, 20, 22, 23)
ROWS = 2048
BLOCK = 256
BLOCKS = ROWS // BLOCK
SLICE = 32
PARTS = 2
VIRTUAL = 26
ABSENT = 27


def trig_table(angles, order, layer):
    lane = lax.broadcasted_iota(jnp.int32, (8, 128), 1)
    theta = jnp.zeros((8, 128), jnp.float32)
    for qubit in range(order.shape[0]):
        theta = jnp.where(lane == qubit, angles[layer, order[qubit]], theta)
    half = 0.5 * theta
    return jnp.cos(half), jnp.sin(half)


def entry(table, qubit):
    return table[0:1, qubit : qubit + 1]


def kron_matrix(trig, qubits, transpose=False):
    cosines, sines = trig
    size = 2 ** len(qubits)
    row = lax.broadcasted_iota(jnp.int32, (size, size), 0)
    column = lax.broadcasted_iota(jnp.int32, (size, size), 1)
    if transpose:
        row, column = column, row
    matrix = None
    for bit, qubit in enumerate(qubits):
        change = (row >> bit & 1) - (column >> bit & 1)
        cosine = jnp.broadcast_to(entry(cosines, qubit), (size, size))
        sine = jnp.broadcast_to(entry(sines, qubit), (size, size))
        factor = jnp.where(change == 0, cosine, jnp.where(change > 0, sine, -sine))
        matrix = factor if matrix is None else matrix * factor
    return matrix


def split(values):
    high = values.astype(jnp.bfloat16)
    low = (values - high.astype(jnp.float32)).astype(jnp.bfloat16)
    return high, low


def row_matrix(trig, qubits):
    small = kron_matrix(trig, qubits[:7])
    cosine, sine = entry(trig[0], qubits[7]), entry(trig[1], qubits[7])
    same, up = small * cosine, small * sine
    matrix = jnp.concatenate(
        [jnp.concatenate([same, -up], axis=1), jnp.concatenate([up, same], axis=1)], axis=0
    )
    return jnp.concatenate(split(matrix), axis=1)


def stacked(left, right):
    left_high, left_low = split(left)
    right_high, right_low = split(right)
    high = jnp.concatenate([left_high, right_high], axis=1)
    low = jnp.concatenate([left_low, right_low], axis=1)
    return jnp.concatenate([high, high, low], axis=0)


def on_rows(matrix, left, right):
    matrix = jnp.concatenate([matrix, matrix[:, :BLOCK]], axis=1)
    both = jnp.dot(matrix, stacked(left, right), preferred_element_type=jnp.float32)
    return both[:, :128], both[:, 128:]


def lane_matrix(trig, qubits):
    return jnp.concatenate(split(kron_matrix(trig, qubits, transpose=True)), axis=1)


def on_lanes(values, matrix):
    high = matrix[:, :128]
    matrix = jnp.concatenate(
        [matrix, jnp.concatenate([high, jnp.zeros_like(high)], axis=1)], axis=0
    )
    parts = jnp.concatenate(split(values), axis=1)
    both = jnp.dot(parts, matrix, preferred_element_type=jnp.float32)
    return both[:, :128] + both[:, 128:]


def butterflies(parts, trig, qubits):
    for bit, qubit in enumerate(qubits):
        cosine, sine = entry(trig[0], qubit), entry(trig[1], qubit)
        out = list(parts)
        for low in range(len(parts)):
            if low >> bit & 1 == 0:
                high = low | 1 << bit
                out[low] = cosine * parts[low] - sine * parts[high]
                out[high] = sine * parts[low] + cosine * parts[high]
        parts = out
    return parts


def lane_indices(pairs, layer, groups):
    lane = lax.broadcasted_iota(jnp.int32, (8, 128), 1)
    result = jnp.full((8, 128), ABSENT, jnp.int32)
    for group, member in enumerate(groups):
        if member is None:
            result = jnp.where(lane >> 5 == group, VIRTUAL, result)
            continue
        for number in range(pairs.shape[2]):
            result = jnp.where(lane == 32 * group + number, pairs[layer, member, number], result)
    return result[0:1]


def features(index, first, second):
    index = index | 1 << VIRTUAL
    return ((index >> first) & (index >> second) & 1).astype(jnp.float32).astype(jnp.bfloat16)


def minus_bits(pairs, layer, first_bit, index_of):
    row_first = lane_indices(pairs, layer, (0, 1, 0, None))
    row_second = lane_indices(pairs, layer, (0, 1, 1, None))
    lane_first = lane_indices(pairs, layer, (1, 0, None, 0))
    lane_second = lane_indices(pairs, layer, (1, 0, None, 1))
    column = lax.broadcasted_iota(jnp.int32, (128, 128), 0)
    right = features(column, lane_first, lane_second)
    row = lax.broadcasted_iota(jnp.int32, (BLOCK, 128), 0)
    bits = jnp.zeros((BLOCK, 128), jnp.int32)
    for block in range(BLOCKS):
        left = features(index_of(block, row), row_first, row_second)
        parity = lax.dot_general(
            left, right, (((1,), (1,)), ((), ())), preferred_element_type=jnp.float32
        )
        bits = bits | (parity.astype(jnp.int32) & 1) << first_bit + block
    return bits


def signed(values, minus, bit):
    return jnp.where(minus & 1 << bit == 0, values, -values)


def fetch(*ways, semaphores):
    copies = [pltpu.make_async_copy(*way, semaphores.at[number]) for number, way in enumerate(ways)]
    for copy in copies:
        copy.start()
    for copy in copies:
        copy.wait()


def place(axes):
    index = 0
    for axis in axes:
        index = index * lax.axis_size(axis) + lax.axis_index(axis)
    return index


def high_bits(peer):
    index = jnp.zeros_like(peer)
    for bit, qubit in enumerate(HIGH):
        index = index | (peer >> bit & 1) << qubit
    return index


def tables_kernel(
    angles_in, order_in, pairs_in, minus, middle, last, lanes, trig_out, angles, order, pairs, small
):
    fetch((angles_in, angles), (order_in, order), (pairs_in, pairs), semaphores=small)
    device = place(AXES)
    peer = place(PEERS)
    first = trig_table(angles, order, 0)
    second = trig_table(angles, order, 1)
    middle[0] = half_matrix(first, HIGH[:7])
    middle[1] = half_matrix(second, HIGH[:7])
    last[...] = row_matrix(second, range(7, 15))
    lanes[...] = lane_matrix(second, range(7))
    trig_out[0], trig_out[1] = first
    trig_out[2], trig_out[3] = second
    middle_bits = minus_bits(
        pairs, 0, 0, lambda block, row: high_bits(row) | peer << 10 | block << 7
    )
    last_bits = minus_bits(
        pairs, 1, BLOCKS, lambda block, row: row + BLOCK * block << 7 | device << 18
    )
    minus[...] = middle_bits | last_bits


def first_kernel(angles_in, order_in, state, out, angles, order, held, scratch, ready, small, arrived, sent):
    copies = []
    for pair in range(BLOCKS // 2):
        blocks = pl.ds(2 * pair, 2)
        copies.append(pltpu.make_async_copy(state.at[blocks], held.at[blocks], arrived.at[pair]))
        copies[-1].start()
    fetch((angles_in, angles), (order_in, order), semaphores=small)
    trig = trig_table(angles, order, 0)
    lanes = lane_matrix(trig, range(7))
    matrix = row_matrix(trig, range(7, 15))
    for copy in copies:
        copy.wait()
    rotate(held, trig, matrix, lanes, None, out, scratch, ready, sent)


def rotate(state, trig, matrix, lanes, minus, out, scratch, ready, sent):
    for start in range(0, BLOCK, SLICE):
        rows = pl.ds(start, SLICE)
        parts = [state[block, rows, :] for block in range(BLOCKS)]
        for block, part in enumerate(butterflies(parts, trig, range(15, 18))):
            scratch[block, rows, :] = part
    turned = [on_lanes(scratch[block], lanes) for block in range(BLOCKS)]
    copies = []
    size = BLOCKS // PARTS
    for part in range(PARTS):
        for here in range(size * part, size * (part + 1), 2):
            for block, values in enumerate(on_rows(matrix, turned[here], turned[here + 1]), here):
                ready[block] = values if minus is None else signed(values, minus, BLOCKS + block)
        blocks = pl.ds(size * part, size)
        copies.append(pltpu.make_async_copy(ready.at[blocks], out.at[blocks], sent.at[part]))
        copies[-1].start()
    for copy in copies:
        copy.wait()


def half_matrix(trig, qubits):
    high, low = split(kron_matrix(trig, qubits))
    return jnp.concatenate(
        [jnp.concatenate([high, high], axis=1), jnp.concatenate([low, jnp.zeros_like(low)], axis=1)],
        axis=0,
    )


def on_half(matrix, values):
    parts = jnp.concatenate(split(values), axis=0)
    both = jnp.dot(matrix, parts, preferred_element_type=jnp.float32)
    return both[:128] + both[128:]


def second_kernel(minus, matrices, trig, state, out):
    first, second = (trig[0], trig[1]), (trig[2], trig[3])
    sides = range(2)

    def rows(row, half):
        return pl.ds(row + 8 * 128 * half, 128, stride=8)

    turned = []
    for here in range(0, 8, 2):
        halves = []
        for half in sides:
            both = jnp.concatenate([state[rows(here + side, half), :] for side in sides], axis=1)
            halves.append(on_half(matrices[0], both))
        halves = butterflies(halves, first, HIGH[7:])
        for half in sides:
            bits = minus[pl.ds(128 * half, 128), :]
            both = halves[half][:, :128], halves[half][:, 128:]
            both = [signed(values, bits, here + side) for side, values in enumerate(both)]
            halves[half] = jnp.concatenate(both, axis=1)
        turned.append(butterflies(halves, second, HIGH[7:]))
    for here in range(0, 8, 2):
        for half in sides:
            both = on_half(matrices[1], turned[here // 2][half])
            out[rows(here, half), :], out[rows(here + 1, half), :] = both[:, :128], both[:, 128:]


def third_kernel(minus, matrix, lanes, trig, state, out, scratch, ready, sent):
    trig = trig[2], trig[3]
    rotate(state, trig, matrix[...], lanes[...], minus[...], out, scratch, ready, sent)


HELD = pltpu.VMEM((ROWS, 128), jnp.float32)
IN_BLOCKS = pltpu.VMEM((BLOCKS, BLOCK, 128), jnp.float32)
PARAMS = pltpu.CompilerParams(vmem_limit_bytes=12 * 2**20)
VMEM, SMEM, HBM = (pl.BlockSpec(memory_space=space) for space in (pltpu.VMEM, pltpu.SMEM, pltpu.HBM))


def in_hbm(array):
    return pltpu.with_memory_space_constraint(array, pltpu.HBM)


def make_tables(angles, order, pairs):
    return pl.pallas_call(
        tables_kernel,
        out_shape=(
            pltpu.VMEM((BLOCK, 128), jnp.int32),
            pltpu.VMEM((2, 256, 256), jnp.bfloat16),
            pltpu.VMEM((256, 512), jnp.bfloat16),
            pltpu.VMEM((128, 256), jnp.bfloat16),
            pltpu.VMEM((4, 8, 128), jnp.float32),
        ),
        in_specs=[HBM] * 3,
        out_specs=(VMEM,) * 5,
        scratch_shapes=[
            pltpu.SMEM(angles.shape, jnp.float32),
            pltpu.SMEM(order.shape, jnp.int32),
            pltpu.SMEM(pairs.shape, jnp.int32),
            pltpu.SemaphoreType.DMA((3,)),
        ],
        compiler_params=PARAMS,
    )(*(in_hbm(array) for array in (angles, order, pairs)))


def first(angles, order, state):
    state = state.reshape(IN_BLOCKS.shape)
    return pl.pallas_call(
        first_kernel,
        out_shape=pltpu.HBM(IN_BLOCKS.shape, jnp.float32),
        in_specs=[HBM] * 3,
        out_specs=HBM,
        scratch_shapes=[
            pltpu.SMEM(angles.shape, jnp.float32),
            pltpu.SMEM(order.shape, jnp.int32),
            IN_BLOCKS,
            IN_BLOCKS,
            IN_BLOCKS,
            pltpu.SemaphoreType.DMA((2,)),
            pltpu.SemaphoreType.DMA((BLOCKS // 2,)),
            pltpu.SemaphoreType.DMA((PARTS,)),
        ],
        compiler_params=PARAMS,
    )(*(in_hbm(array) for array in (angles, order, state))).reshape(ROWS, 128)


def second(minus, matrices, trig, state):
    return pl.pallas_call(
        second_kernel, out_shape=HELD, in_specs=[VMEM] * 4, out_specs=VMEM, compiler_params=PARAMS
    )(minus, matrices, trig, state)


def third(minus, matrix, lanes, trig, state):
    return pl.pallas_call(
        third_kernel,
        out_shape=jax.ShapeDtypeStruct(IN_BLOCKS.shape, jnp.float32),
        in_specs=[VMEM] * 5,
        out_specs=HBM,
        scratch_shapes=[IN_BLOCKS, IN_BLOCKS, pltpu.SemaphoreType.DMA((PARTS,))],
        compiler_params=PARAMS,
    )(minus, matrix, lanes, trig, state.reshape(IN_BLOCKS.shape))


def exchange(state):
    chunks = state.reshape(256, 8, 128)
    return lax.all_to_all(chunks, PEERS, 0, 0, tiled=True).reshape(ROWS, 128)


def local(state_slab, angles, qubit_order, entangler_pairs):
    minus, middle, last, lanes, trig = make_tables(
        angles, qubit_order, entangler_pairs.transpose(0, 2, 1)
    )
    state = first(angles, qubit_order, state_slab.reshape(ROWS, 128))
    state = exchange(state)
    state = second(minus, middle, trig, state)
    state = exchange(state)
    state = third(minus, last, lanes, trig, state)
    return state.reshape(state_slab.shape)


def solution(mesh):
    in_specs = (P(AXES, None), P(), P(), P())
    mesh = Mesh(mesh.devices.reshape(SIZES), AXES)
    return jax.shard_map(local, mesh=mesh, in_specs=in_specs, out_specs=P(AXES, None), check_vma=False)
```

```python
import functools

import jax
import jax.numpy as jnp
from jax import lax
from jax.experimental import pallas as pl
from jax.experimental.pallas import tpu as pltpu
from jax.sharding import Mesh
from jax.sharding import PartitionSpec as P

AXIS = "device"
PEERS = [
    x << 6 | z >> 1 << 4 | core << 3 | (z & 1) << 2 | y
    for z in range(8)
    for y in range(4)
    for x in range(4)
    for core in range(2)
]
HIGH = (21, 24, 25, 18, 19, 20, 22, 23)
ROWS = 2048
BLOCK = 256
BLOCKS = ROWS // BLOCK
SLICE = 32
PARTS = 2
VIRTUAL = 26
ABSENT = 27


def trig_table(angles, order, layer):
    lane = lax.broadcasted_iota(jnp.int32, (8, 128), 1)
    theta = jnp.zeros((8, 128), jnp.float32)
    for qubit in range(order.shape[0]):
        theta = jnp.where(lane == qubit, angles[layer, order[qubit]], theta)
    half = 0.5 * theta
    return jnp.cos(half), jnp.sin(half)


def entry(table, qubit):
    return table[0:1, qubit : qubit + 1]


def kron_matrix(trig, qubits, transpose=False, backwards=False):
    cosines, sines = trig
    size = 2 ** len(qubits)
    row = lax.broadcasted_iota(jnp.int32, (size, size), 0)
    column = lax.broadcasted_iota(jnp.int32, (size, size), 1)
    if backwards:
        row = size - 1 - row
    if transpose:
        row, column = column, row
    matrix = None
    for bit, qubit in enumerate(qubits):
        change = (row >> bit & 1) - (column >> bit & 1)
        cosine = jnp.broadcast_to(entry(cosines, qubit), (size, size))
        sine = jnp.broadcast_to(entry(sines, qubit), (size, size))
        factor = jnp.where(change == 0, cosine, jnp.where(change > 0, sine, -sine))
        matrix = factor if matrix is None else matrix * factor
    return matrix


def split(values):
    high = values.astype(jnp.bfloat16)
    low = (values - high.astype(jnp.float32)).astype(jnp.bfloat16)
    return high, low


def row_matrix(trig, qubits):
    small = kron_matrix(trig, qubits[:7])
    cosine, sine = entry(trig[0], qubits[7]), entry(trig[1], qubits[7])
    same, up = small * cosine, small * sine
    matrix = jnp.concatenate(
        [jnp.concatenate([same, -up], axis=1), jnp.concatenate([up, same], axis=1)], axis=0
    )
    return jnp.concatenate(split(matrix), axis=1)


def stacked(left, right):
    left_high, left_low = split(left)
    right_high, right_low = split(right)
    high = jnp.concatenate([left_high, right_high], axis=1)
    low = jnp.concatenate([left_low, right_low], axis=1)
    return jnp.concatenate([high, high, low], axis=0)


def on_rows(matrix, left, right):
    matrix = jnp.concatenate([matrix, matrix[:, :BLOCK]], axis=1)
    both = jnp.dot(matrix, stacked(left, right), preferred_element_type=jnp.float32)
    return both[:, :128], both[:, 128:]


def lane_matrix(trig, qubits):
    return jnp.concatenate(split(kron_matrix(trig, qubits, transpose=True)), axis=1)


def on_lanes(values, matrix):
    high = matrix[:, :128]
    matrix = jnp.concatenate(
        [matrix, jnp.concatenate([high, jnp.zeros_like(high)], axis=1)], axis=0
    )
    parts = jnp.concatenate(split(values), axis=1)
    both = jnp.dot(parts, matrix, preferred_element_type=jnp.float32)
    return both[:, :128] + both[:, 128:]


def butterflies(parts, trig, qubits):
    for bit, qubit in enumerate(qubits):
        cosine, sine = entry(trig[0], qubit), entry(trig[1], qubit)
        out = list(parts)
        for low in range(len(parts)):
            if low >> bit & 1 == 0:
                high = low | 1 << bit
                out[low] = cosine * parts[low] - sine * parts[high]
                out[high] = sine * parts[low] + cosine * parts[high]
        parts = out
    return parts


def lane_indices(pairs, layer, groups):
    lane = lax.broadcasted_iota(jnp.int32, (8, 128), 1)
    result = jnp.full((8, 128), ABSENT, jnp.int32)
    for group, member in enumerate(groups):
        if member is None:
            result = jnp.where(lane >> 5 == group, VIRTUAL, result)
            continue
        for number in range(pairs.shape[2]):
            result = jnp.where(lane == 32 * group + number, pairs[layer, member, number], result)
    return result[0:1]


def features(index, first, second):
    index = index | 1 << VIRTUAL
    return ((index >> first) & (index >> second) & 1).astype(jnp.float32).astype(jnp.bfloat16)


def minus_bits(pairs, layer, first_bit, index_of):
    row_first = lane_indices(pairs, layer, (0, 1, 0, None))
    row_second = lane_indices(pairs, layer, (0, 1, 1, None))
    lane_first = lane_indices(pairs, layer, (1, 0, None, 0))
    lane_second = lane_indices(pairs, layer, (1, 0, None, 1))
    column = lax.broadcasted_iota(jnp.int32, (128, 128), 0)
    right = features(column, lane_first, lane_second)
    row = lax.broadcasted_iota(jnp.int32, (BLOCK, 128), 0)
    bits = jnp.zeros((BLOCK, 128), jnp.int32)
    for block in range(BLOCKS):
        left = features(index_of(block, row), row_first, row_second)
        parity = lax.dot_general(
            left, right, (((1,), (1,)), ((), ())), preferred_element_type=jnp.float32
        )
        bits = bits | (parity.astype(jnp.int32) & 1) << first_bit + block
    return bits


def signed(values, minus, bit):
    return jnp.where(minus & 1 << bit == 0, values, -values)


def fetch(*ways, semaphores):
    copies = [pltpu.make_async_copy(*way, semaphores.at[number]) for number, way in enumerate(ways)]
    for copy in copies:
        copy.start()
    for copy in copies:
        copy.wait()


def peer_of(device):
    z = device >> 3 & 6 | device >> 2 & 1
    return z << 5 | (device & 3) << 3 | device >> 6 << 1 | device >> 3 & 1


def high_bits(peer):
    index = jnp.zeros_like(peer)
    for bit, qubit in enumerate(HIGH):
        index = index | (peer >> bit & 1) << qubit
    return index


def tables_kernel(
    angles_in, order_in, pairs_in, minus, middle, last, lanes, trig_out, angles, order, pairs, small
):
    fetch((angles_in, angles), (order_in, order), (pairs_in, pairs), semaphores=small)
    device = lax.axis_index(AXIS)
    peer = peer_of(device)
    first = trig_table(angles, order, 0)
    second = trig_table(angles, order, 1)
    middle[0] = half_matrix(first, HIGH[:7])
    middle[1] = half_matrix(second, HIGH[:7], backwards=True)
    last[...] = row_matrix(second, range(7, 15))
    lanes[...] = lane_matrix(second, range(7))
    trig_out[0], trig_out[1] = first
    trig_out[2], trig_out[3] = second
    middle_bits = minus_bits(
        pairs, 0, 0, lambda block, row: high_bits(row) | peer << 10 | block << 7
    )
    last_bits = minus_bits(
        pairs, 1, BLOCKS, lambda block, row: row + BLOCK * block << 7 | device << 18
    )
    minus[...] = middle_bits | last_bits


def first_kernel(angles_in, order_in, state, out, angles, order, held, scratch, ready, small, arrived, sent):
    copies = []
    for pair in range(BLOCKS // 2):
        blocks = pl.ds(2 * pair, 2)
        copies.append(pltpu.make_async_copy(state.at[blocks], held.at[blocks], arrived.at[pair]))
        copies[-1].start()
    fetch((angles_in, angles), (order_in, order), semaphores=small)
    trig = trig_table(angles, order, 0)
    lanes = lane_matrix(trig, range(7))
    matrix = row_matrix(trig, range(7, 15))
    for copy in copies:
        copy.wait()
    rotate(held, slice_of, trig, matrix, lanes, None, out, scratch, ready, sent)


def slice_of(state, block, start):
    return state[block, pl.ds(start, SLICE), :]


def slice_backwards(state, block, start):
    chunk = (BLOCK * block + start) // 8
    return jnp.concatenate([state[255 - chunk - part] for part in range(SLICE // 8)], axis=0)


def rotate(state, load, trig, matrix, lanes, minus, out, scratch, ready, sent):
    for start in range(0, BLOCK, SLICE):
        rows = pl.ds(start, SLICE)
        parts = [load(state, block, start) for block in range(BLOCKS)]
        for block, part in enumerate(butterflies(parts, trig, range(15, 18))):
            scratch[block, rows, :] = part
    turned = [on_lanes(scratch[block], lanes) for block in range(BLOCKS)]
    copies = []
    size = BLOCKS // PARTS
    for part in range(PARTS):
        for here in range(size * part, size * (part + 1), 2):
            for block, values in enumerate(on_rows(matrix, turned[here], turned[here + 1]), here):
                ready[block] = values if minus is None else signed(values, minus, BLOCKS + block)
        blocks = pl.ds(size * part, size)
        copies.append(pltpu.make_async_copy(ready.at[blocks], out.at[blocks], sent.at[part]))
        copies[-1].start()
    for copy in copies:
        copy.wait()


def half_matrix(trig, qubits, backwards=False):
    high, low = split(kron_matrix(trig, qubits, backwards=backwards))
    return jnp.concatenate(
        [jnp.concatenate([high, high], axis=1), jnp.concatenate([low, jnp.zeros_like(low)], axis=1)],
        axis=0,
    )


def on_half(matrix, values):
    parts = jnp.concatenate(split(values), axis=0)
    both = jnp.dot(matrix, parts, preferred_element_type=jnp.float32)
    return both[:128] + both[128:]


def second_kernel(minus, matrices, trig, state, out):
    first, second = (trig[0], trig[1]), (trig[2], trig[3])
    sides = range(2)

    def rows(row, half):
        return pl.ds(row + 8 * 128 * half, 128, stride=8)

    turned = []
    for here in range(0, 8, 2):
        halves = []
        for half in sides:
            both = jnp.concatenate([state[rows(here + side, half), :] for side in sides], axis=1)
            halves.append(on_half(matrices[0], both))
        halves = butterflies(halves, first, HIGH[7:])
        for half in sides:
            bits = minus[pl.ds(128 * half, 128), :]
            both = halves[half][:, :128], halves[half][:, 128:]
            both = [signed(values, bits, here + side) for side, values in enumerate(both)]
            halves[half] = jnp.concatenate(both, axis=1)
        turned.append(butterflies(halves, second, HIGH[7:]))
    for here in range(0, 8, 2):
        for half in sides:
            both = on_half(matrices[1], turned[here // 2][half])
            out[rows(here, 1 - half), :], out[rows(here + 1, 1 - half), :] = both[:, :128], both[:, 128:]


def third_kernel(minus, matrix, lanes, trig, state, out, scratch, ready, sent):
    trig = trig[2], trig[3]
    rotate(state, slice_backwards, trig, matrix[...], lanes[...], minus[...], out, scratch, ready, sent)


HELD = pltpu.VMEM((ROWS, 128), jnp.float32)
IN_BLOCKS = pltpu.VMEM((BLOCKS, BLOCK, 128), jnp.float32)
PARAMS = pltpu.CompilerParams(vmem_limit_bytes=12 * 2**20)
VMEM, SMEM, HBM = (pl.BlockSpec(memory_space=space) for space in (pltpu.VMEM, pltpu.SMEM, pltpu.HBM))


def in_hbm(array):
    return pltpu.with_memory_space_constraint(array, pltpu.HBM)


def make_tables(angles, order, pairs):
    return pl.pallas_call(
        tables_kernel,
        out_shape=(
            pltpu.VMEM((BLOCK, 128), jnp.int32),
            pltpu.VMEM((2, 256, 256), jnp.bfloat16),
            pltpu.VMEM((256, 512), jnp.bfloat16),
            pltpu.VMEM((128, 256), jnp.bfloat16),
            pltpu.VMEM((4, 8, 128), jnp.float32),
        ),
        in_specs=[HBM] * 3,
        out_specs=(VMEM,) * 5,
        scratch_shapes=[
            pltpu.SMEM(angles.shape, jnp.float32),
            pltpu.SMEM(order.shape, jnp.int32),
            pltpu.SMEM(pairs.shape, jnp.int32),
            pltpu.SemaphoreType.DMA((3,)),
        ],
        compiler_params=PARAMS,
    )(*(in_hbm(array) for array in (angles, order, pairs)))


def first(angles, order, state):
    state = state.reshape(IN_BLOCKS.shape)
    return pl.pallas_call(
        first_kernel,
        out_shape=pltpu.HBM(IN_BLOCKS.shape, jnp.float32),
        in_specs=[HBM] * 3,
        out_specs=HBM,
        scratch_shapes=[
            pltpu.SMEM(angles.shape, jnp.float32),
            pltpu.SMEM(order.shape, jnp.int32),
            IN_BLOCKS,
            IN_BLOCKS,
            IN_BLOCKS,
            pltpu.SemaphoreType.DMA((2,)),
            pltpu.SemaphoreType.DMA((BLOCKS // 2,)),
            pltpu.SemaphoreType.DMA((PARTS,)),
        ],
        compiler_params=PARAMS,
    )(*(in_hbm(array) for array in (angles, order, state))).reshape(ROWS, 128)


def second(minus, matrices, trig, state):
    return pl.pallas_call(
        second_kernel, out_shape=HELD, in_specs=[VMEM] * 4, out_specs=VMEM, compiler_params=PARAMS
    )(minus, matrices, trig, state)


def third(minus, matrix, lanes, trig, state):
    return pl.pallas_call(
        third_kernel,
        out_shape=jax.ShapeDtypeStruct(IN_BLOCKS.shape, jnp.float32),
        in_specs=[VMEM] * 5,
        out_specs=HBM,
        scratch_shapes=[IN_BLOCKS, IN_BLOCKS, pltpu.SemaphoreType.DMA((PARTS,))],
        compiler_params=PARAMS,
    )(minus, matrix, lanes, trig, state.reshape(256, 8, 128))


def exchange(state, peers):
    chunks = state.reshape(256, 8, 128)
    return lax.all_to_all(chunks, AXIS, 0, 0, axis_index_groups=[peers], tiled=True).reshape(ROWS, 128)


def local(state_slab, angles, qubit_order, entangler_pairs):
    minus, middle, last, lanes, trig = make_tables(
        angles, qubit_order, entangler_pairs.transpose(0, 2, 1)
    )
    state = first(angles, qubit_order, state_slab.reshape(ROWS, 128))
    state = exchange(state, PEERS)
    state = second(minus, middle, trig, state)
    state = exchange(state, PEERS[::-1])
    state = third(minus, last, lanes, trig, state)
    return state.reshape(state_slab.shape)


def solution(mesh):
    in_specs = (P(AXIS, None), P(), P(), P())
    mesh = Mesh(mesh.devices.reshape(-1), (AXIS,))
    return jax.shard_map(local, mesh=mesh, in_specs=in_specs, out_specs=P(AXIS, None), check_vma=False)
```

```python
import functools

import jax
import jax.numpy as jnp
from jax import lax
from jax.experimental import pallas as pl
from jax.experimental.pallas import tpu as pltpu
from jax.sharding import Mesh
from jax.sharding import PartitionSpec as P

AXIS = "device"
PEERS = [
    x << 6 | z >> 1 << 4 | core << 3 | (z & 1) << 2 | y
    for z in range(8)
    for y in range(4)
    for x in range(4)
    for core in range(2)
]
HIGH = (21, 24, 25, 18, 19, 20, 22, 23)
ROWS = 2048
BLOCK = 256
BLOCKS = ROWS // BLOCK
SLICE = 32
PARTS = 2
VIRTUAL = 26
ABSENT = 27


def trig_table(angles, order, layer):
    lane = lax.broadcasted_iota(jnp.int32, (8, 128), 1)
    theta = jnp.zeros((8, 128), jnp.float32)
    for qubit in range(order.shape[0]):
        theta = jnp.where(lane == qubit, angles[layer, order[qubit]], theta)
    half = 0.5 * theta
    return jnp.cos(half), jnp.sin(half)


def entry(table, qubit):
    return table[0:1, qubit : qubit + 1]


def kron_matrix(trig, qubits, transpose=False, backwards=False):
    cosines, sines = trig
    size = 2 ** len(qubits)
    row = lax.broadcasted_iota(jnp.int32, (size, size), 0)
    column = lax.broadcasted_iota(jnp.int32, (size, size), 1)
    if backwards:
        row = size - 1 - row
    if transpose:
        row, column = column, row
    matrix = None
    for bit, qubit in enumerate(qubits):
        change = (row >> bit & 1) - (column >> bit & 1)
        cosine = jnp.broadcast_to(entry(cosines, qubit), (size, size))
        sine = jnp.broadcast_to(entry(sines, qubit), (size, size))
        factor = jnp.where(change == 0, cosine, jnp.where(change > 0, sine, -sine))
        matrix = factor if matrix is None else matrix * factor
    return matrix


def split(values):
    high = values.astype(jnp.bfloat16)
    low = (values - high.astype(jnp.float32)).astype(jnp.bfloat16)
    return high, low


def lane_matrix(trig, qubits):
    return jnp.concatenate(split(kron_matrix(trig, qubits, transpose=True)), axis=1)


def on_lanes(values, matrix):
    high = matrix[:, :128]
    matrix = jnp.concatenate(
        [matrix, jnp.concatenate([high, jnp.zeros_like(high)], axis=1)], axis=0
    )
    parts = jnp.concatenate(split(values), axis=1)
    both = jnp.dot(parts, matrix, preferred_element_type=jnp.float32)
    return both[:, :128] + both[:, 128:]


def butterflies(parts, trig, qubits):
    for bit, qubit in enumerate(qubits):
        cosine, sine = entry(trig[0], qubit), entry(trig[1], qubit)
        out = list(parts)
        for low in range(len(parts)):
            if low >> bit & 1 == 0:
                high = low | 1 << bit
                out[low] = cosine * parts[low] - sine * parts[high]
                out[high] = sine * parts[low] + cosine * parts[high]
        parts = out
    return parts


def lane_indices(pairs, layer, groups):
    lane = lax.broadcasted_iota(jnp.int32, (8, 128), 1)
    result = jnp.full((8, 128), ABSENT, jnp.int32)
    for group, member in enumerate(groups):
        if member is None:
            result = jnp.where(lane >> 5 == group, VIRTUAL, result)
            continue
        for number in range(pairs.shape[2]):
            result = jnp.where(lane == 32 * group + number, pairs[layer, member, number], result)
    return result[0:1]


def features(index, first, second):
    index = index | 1 << VIRTUAL
    return ((index >> first) & (index >> second) & 1).astype(jnp.float32).astype(jnp.bfloat16)


def minus_bits(pairs, layer, first_bit, index_of):
    row_first = lane_indices(pairs, layer, (0, 1, 0, None))
    row_second = lane_indices(pairs, layer, (0, 1, 1, None))
    lane_first = lane_indices(pairs, layer, (1, 0, None, 0))
    lane_second = lane_indices(pairs, layer, (1, 0, None, 1))
    column = lax.broadcasted_iota(jnp.int32, (128, 128), 0)
    right = features(column, lane_first, lane_second)
    row = lax.broadcasted_iota(jnp.int32, (BLOCK, 128), 0)
    bits = jnp.zeros((BLOCK, 128), jnp.int32)
    for block in range(BLOCKS):
        left = features(index_of(block, row), row_first, row_second)
        parity = lax.dot_general(
            left, right, (((1,), (1,)), ((), ())), preferred_element_type=jnp.float32
        )
        bits = bits | (parity.astype(jnp.int32) & 1) << first_bit + block
    return bits


def signed(values, minus, bit):
    return jnp.where(minus & 1 << bit == 0, values, -values)


def fetch(*ways, semaphores):
    copies = [pltpu.make_async_copy(*way, semaphores.at[number]) for number, way in enumerate(ways)]
    for copy in copies:
        copy.start()
    for copy in copies:
        copy.wait()


def peer_of(device):
    z = device >> 3 & 6 | device >> 2 & 1
    return z << 5 | (device & 3) << 3 | device >> 6 << 1 | device >> 3 & 1


def high_bits(peer):
    index = jnp.zeros_like(peer)
    for bit, qubit in enumerate(HIGH):
        index = index | (peer >> bit & 1) << qubit
    return index


def tables_kernel(
    angles_in, order_in, pairs_in, minus, middle, last, lanes, trig_out, angles, order, pairs, small
):
    fetch((angles_in, angles), (order_in, order), (pairs_in, pairs), semaphores=small)
    device = lax.axis_index(AXIS)
    peer = peer_of(device)
    first = trig_table(angles, order, 0)
    second = trig_table(angles, order, 1)
    middle[0] = half_matrix(first, HIGH[:7])
    middle[1] = half_matrix(second, HIGH[:7], backwards=True)
    last[...] = half_matrix(second, range(7, 14))
    lanes[...] = lane_matrix(second, range(7))
    trig_out[0], trig_out[1] = first
    trig_out[2], trig_out[3] = second
    middle_bits = minus_bits(
        pairs, 0, 0, lambda block, row: high_bits(row) | peer << 10 | block << 7
    )
    last_bits = minus_bits(
        pairs, 1, BLOCKS, lambda block, row: row + BLOCK * block << 7 | device << 18
    )
    minus[...] = middle_bits | last_bits


def first_kernel(angles_in, order_in, state, out, angles, order, held, scratch, ready, small, arrived, sent):
    copies = []
    for pair in range(BLOCKS // 2):
        blocks = pl.ds(2 * pair, 2)
        copies.append(pltpu.make_async_copy(state.at[blocks], held.at[blocks], arrived.at[pair]))
        copies[-1].start()
    fetch((angles_in, angles), (order_in, order), semaphores=small)
    trig = trig_table(angles, order, 0)
    lanes = lane_matrix(trig, range(7))
    matrix = half_matrix(trig, range(7, 14))
    for copy in copies:
        copy.wait()
    rotate(held, slice_of, trig, matrix, lanes, None, out, scratch, ready, sent)


def slice_of(state, block, start):
    return state[block, pl.ds(start, SLICE), :]


def slice_backwards(state, block, start):
    chunk = (BLOCK * block + start) // 8
    return jnp.concatenate([state[255 - chunk - part] for part in range(SLICE // 8)], axis=0)


def rotate(state, load, trig, matrix, lanes, minus, out, scratch, ready, sent):
    for start in range(0, BLOCK, SLICE):
        rows = pl.ds(start, SLICE)
        parts = [load(state, block, start) for block in range(BLOCKS)]
        for block, part in enumerate(butterflies(parts, trig, range(15, 18))):
            scratch[block, rows, :] = part
    turned = [on_lanes(scratch[block], lanes) for block in range(BLOCKS)]
    copies = []
    size = BLOCKS // PARTS
    for part in range(PARTS):
        for here in range(size * part, size * (part + 1), 2):
            both = jnp.concatenate(turned[here : here + 2], axis=1)
            halves = [on_half(matrix, both[:128]), on_half(matrix, both[128:])]
            halves = butterflies(halves, trig, range(14, 15))
            both = jnp.concatenate(halves, axis=0)
            for block, values in enumerate((both[:, :128], both[:, 128:]), here):
                ready[block] = values if minus is None else signed(values, minus, BLOCKS + block)
        blocks = pl.ds(size * part, size)
        copies.append(pltpu.make_async_copy(ready.at[blocks], out.at[blocks], sent.at[part]))
        copies[-1].start()
    for copy in copies:
        copy.wait()


def half_matrix(trig, qubits, backwards=False):
    high, low = split(kron_matrix(trig, qubits, backwards=backwards))
    return jnp.concatenate(
        [jnp.concatenate([high, high], axis=1), jnp.concatenate([low, jnp.zeros_like(low)], axis=1)],
        axis=0,
    )


def on_half(matrix, values):
    parts = jnp.concatenate(split(values), axis=0)
    both = jnp.dot(matrix, parts, preferred_element_type=jnp.float32)
    return both[:128] + both[128:]


def second_kernel(minus, matrices, trig, state, out):
    first, second = (trig[0], trig[1]), (trig[2], trig[3])
    sides = range(2)

    def rows(row, half):
        return pl.ds(row + 8 * 128 * half, 128, stride=8)

    turned = []
    for here in range(0, 8, 2):
        halves = []
        for half in sides:
            both = jnp.concatenate([state[rows(here + side, half), :] for side in sides], axis=1)
            halves.append(on_half(matrices[0], both))
        halves = butterflies(halves, first, HIGH[7:])
        for half in sides:
            bits = minus[pl.ds(128 * half, 128), :]
            both = halves[half][:, :128], halves[half][:, 128:]
            both = [signed(values, bits, here + side) for side, values in enumerate(both)]
            halves[half] = jnp.concatenate(both, axis=1)
        turned.append(butterflies(halves, second, HIGH[7:]))
    for here in range(0, 8, 2):
        for half in sides:
            both = on_half(matrices[1], turned[here // 2][half])
            out[rows(here, 1 - half), :], out[rows(here + 1, 1 - half), :] = both[:, :128], both[:, 128:]


def third_kernel(minus, matrix, lanes, trig, state, out, scratch, ready, sent):
    trig = trig[2], trig[3]
    rotate(state, slice_backwards, trig, matrix[...], lanes[...], minus[...], out, scratch, ready, sent)


HELD = pltpu.VMEM((ROWS, 128), jnp.float32)
IN_BLOCKS = pltpu.VMEM((BLOCKS, BLOCK, 128), jnp.float32)
PARAMS = pltpu.CompilerParams(vmem_limit_bytes=12 * 2**20)
VMEM, SMEM, HBM = (pl.BlockSpec(memory_space=space) for space in (pltpu.VMEM, pltpu.SMEM, pltpu.HBM))


def in_hbm(array):
    return pltpu.with_memory_space_constraint(array, pltpu.HBM)


def make_tables(angles, order, pairs):
    return pl.pallas_call(
        tables_kernel,
        out_shape=(
            pltpu.VMEM((BLOCK, 128), jnp.int32),
            pltpu.VMEM((2, 256, 256), jnp.bfloat16),
            pltpu.VMEM((256, 256), jnp.bfloat16),
            pltpu.VMEM((128, 256), jnp.bfloat16),
            pltpu.VMEM((4, 8, 128), jnp.float32),
        ),
        in_specs=[HBM] * 3,
        out_specs=(VMEM,) * 5,
        scratch_shapes=[
            pltpu.SMEM(angles.shape, jnp.float32),
            pltpu.SMEM(order.shape, jnp.int32),
            pltpu.SMEM(pairs.shape, jnp.int32),
            pltpu.SemaphoreType.DMA((3,)),
        ],
        compiler_params=PARAMS,
    )(*(in_hbm(array) for array in (angles, order, pairs)))


def first(angles, order, state):
    state = state.reshape(IN_BLOCKS.shape)
    return pl.pallas_call(
        first_kernel,
        out_shape=pltpu.HBM(IN_BLOCKS.shape, jnp.float32),
        in_specs=[HBM] * 3,
        out_specs=HBM,
        scratch_shapes=[
            pltpu.SMEM(angles.shape, jnp.float32),
            pltpu.SMEM(order.shape, jnp.int32),
            IN_BLOCKS,
            IN_BLOCKS,
            IN_BLOCKS,
            pltpu.SemaphoreType.DMA((2,)),
            pltpu.SemaphoreType.DMA((BLOCKS // 2,)),
            pltpu.SemaphoreType.DMA((PARTS,)),
        ],
        compiler_params=PARAMS,
    )(*(in_hbm(array) for array in (angles, order, state))).reshape(ROWS, 128)


def second(minus, matrices, trig, state):
    return pl.pallas_call(
        second_kernel, out_shape=HELD, in_specs=[VMEM] * 4, out_specs=VMEM, compiler_params=PARAMS
    )(minus, matrices, trig, state)


def third(minus, matrix, lanes, trig, state):
    return pl.pallas_call(
        third_kernel,
        out_shape=jax.ShapeDtypeStruct(IN_BLOCKS.shape, jnp.float32),
        in_specs=[VMEM] * 5,
        out_specs=HBM,
        scratch_shapes=[IN_BLOCKS, IN_BLOCKS, pltpu.SemaphoreType.DMA((PARTS,))],
        compiler_params=PARAMS,
    )(minus, matrix, lanes, trig, state.reshape(256, 8, 128))


def exchange(state, peers):
    chunks = state.reshape(256, 8, 128)
    return lax.all_to_all(chunks, AXIS, 0, 0, axis_index_groups=[peers], tiled=True).reshape(ROWS, 128)


def local(state_slab, angles, qubit_order, entangler_pairs):
    minus, middle, last, lanes, trig = make_tables(
        angles, qubit_order, entangler_pairs.transpose(0, 2, 1)
    )
    state = first(angles, qubit_order, state_slab.reshape(ROWS, 128))
    state = exchange(state, PEERS)
    state = second(minus, middle, trig, state)
    state = exchange(state, PEERS[::-1])
    state = third(minus, last, lanes, trig, state)
    return state.reshape(state_slab.shape)


def solution(mesh):
    in_specs = (P(AXIS, None), P(), P(), P())
    mesh = Mesh(mesh.devices.reshape(-1), (AXIS,))
    return jax.shard_map(local, mesh=mesh, in_specs=in_specs, out_specs=P(AXIS, None), check_vma=False)
```

```python
import functools

import jax
import jax.numpy as jnp
from jax import lax
from jax.experimental import pallas as pl
from jax.experimental.pallas import tpu as pltpu
from jax.sharding import Mesh
from jax.sharding import PartitionSpec as P

AXIS = "device"
PEERS = [
    x << 6 | z >> 1 << 4 | core << 3 | (z & 1) << 2 | y
    for z in range(8)
    for y in range(4)
    for x in range(4)
    for core in range(2)
]
HIGH = (21, 24, 25, 18, 19, 20, 22, 23)
ROWS = 2048
BLOCK = 256
BLOCKS = ROWS // BLOCK
SLICE = 16
PARTS = 2
VIRTUAL = 26
ABSENT = 27


def trig_table(angles, order, layer):
    lane = lax.broadcasted_iota(jnp.int32, (8, 128), 1)
    theta = jnp.zeros((8, 128), jnp.float32)
    for qubit in range(order.shape[0]):
        theta = jnp.where(lane == qubit, angles[layer, order[qubit]], theta)
    half = 0.5 * theta
    return jnp.cos(half), jnp.sin(half)


def entry(table, qubit):
    return table[0:1, qubit : qubit + 1]


def kron_matrix(trig, qubits, transpose=False, backwards=False):
    cosines, sines = trig
    size = 2 ** len(qubits)
    row = lax.broadcasted_iota(jnp.int32, (size, size), 0)
    column = lax.broadcasted_iota(jnp.int32, (size, size), 1)
    if backwards:
        row = size - 1 - row
    if transpose:
        row, column = column, row
    matrix = None
    for bit, qubit in enumerate(qubits):
        change = (row >> bit & 1) - (column >> bit & 1)
        cosine = jnp.broadcast_to(entry(cosines, qubit), (size, size))
        sine = jnp.broadcast_to(entry(sines, qubit), (size, size))
        factor = jnp.where(change == 0, cosine, jnp.where(change > 0, sine, -sine))
        matrix = factor if matrix is None else matrix * factor
    return matrix


def split(values):
    high = values.astype(jnp.bfloat16)
    low = (values - high.astype(jnp.float32)).astype(jnp.bfloat16)
    return high, low


def row_matrix(trig, qubits):
    small = kron_matrix(trig, qubits[:7])
    cosine, sine = entry(trig[0], qubits[7]), entry(trig[1], qubits[7])
    same, up = small * cosine, small * sine
    matrix = jnp.concatenate(
        [jnp.concatenate([same, -up], axis=1), jnp.concatenate([up, same], axis=1)], axis=0
    )
    return jnp.concatenate(split(matrix), axis=1)


def stacked(left, right):
    left_high, left_low = split(left)
    right_high, right_low = split(right)
    high = jnp.concatenate([left_high, right_high], axis=1)
    low = jnp.concatenate([left_low, right_low], axis=1)
    return jnp.concatenate([high, high, low], axis=0)


def on_rows(matrix, left, right):
    matrix = jnp.concatenate([matrix, matrix[:, :BLOCK]], axis=1)
    both = jnp.dot(matrix, stacked(left, right), preferred_element_type=jnp.float32)
    return both[:, :128], both[:, 128:]


def lane_matrix(trig, qubits):
    return jnp.concatenate(split(kron_matrix(trig, qubits, transpose=True)), axis=1)


def on_lanes(values, matrix):
    high = matrix[:, :128]
    matrix = jnp.concatenate(
        [matrix, jnp.concatenate([high, jnp.zeros_like(high)], axis=1)], axis=0
    )
    parts = jnp.concatenate(split(values), axis=1)
    both = jnp.dot(parts, matrix, preferred_element_type=jnp.float32)
    return both[:, :128] + both[:, 128:]


def butterflies(parts, trig, qubits):
    for bit, qubit in enumerate(qubits):
        cosine, sine = entry(trig[0], qubit), entry(trig[1], qubit)
        out = list(parts)
        for low in range(len(parts)):
            if low >> bit & 1 == 0:
                high = low | 1 << bit
                out[low] = cosine * parts[low] - sine * parts[high]
                out[high] = sine * parts[low] + cosine * parts[high]
        parts = out
    return parts


def lane_indices(pairs, layer, groups):
    lane = lax.broadcasted_iota(jnp.int32, (8, 128), 1)
    result = jnp.full((8, 128), ABSENT, jnp.int32)
    for group, member in enumerate(groups):
        if member is None:
            result = jnp.where(lane >> 5 == group, VIRTUAL, result)
            continue
        for number in range(pairs.shape[2]):
            result = jnp.where(lane == 32 * group + number, pairs[layer, member, number], result)
    return result[0:1]


def features(index, first, second):
    index = index | 1 << VIRTUAL
    return ((index >> first) & (index >> second) & 1).astype(jnp.float32).astype(jnp.bfloat16)


def minus_bits(pairs, layer, first_bit, index_of):
    row_first = lane_indices(pairs, layer, (0, 1, 0, None))
    row_second = lane_indices(pairs, layer, (0, 1, 1, None))
    lane_first = lane_indices(pairs, layer, (1, 0, None, 0))
    lane_second = lane_indices(pairs, layer, (1, 0, None, 1))
    column = lax.broadcasted_iota(jnp.int32, (128, 128), 0)
    right = features(column, lane_first, lane_second)
    row = lax.broadcasted_iota(jnp.int32, (BLOCK, 128), 0)
    bits = jnp.zeros((BLOCK, 128), jnp.int32)
    for block in range(BLOCKS):
        left = features(index_of(block, row), row_first, row_second)
        parity = lax.dot_general(
            left, right, (((1,), (1,)), ((), ())), preferred_element_type=jnp.float32
        )
        bits = bits | (parity.astype(jnp.int32) & 1) << first_bit + block
    return bits


def signed(values, minus, bit):
    return jnp.where(minus & 1 << bit == 0, values, -values)


def fetch(*ways, semaphores):
    copies = [pltpu.make_async_copy(*way, semaphores.at[number]) for number, way in enumerate(ways)]
    for copy in copies:
        copy.start()
    for copy in copies:
        copy.wait()


def peer_of(device):
    z = device >> 3 & 6 | device >> 2 & 1
    return z << 5 | (device & 3) << 3 | device >> 6 << 1 | device >> 3 & 1


def high_bits(peer):
    index = jnp.zeros_like(peer)
    for bit, qubit in enumerate(HIGH):
        index = index | (peer >> bit & 1) << qubit
    return index


def tables_kernel(
    angles_in, order_in, pairs_in, minus, middle, last, lanes, trig_out, angles, order, pairs, small
):
    fetch((angles_in, angles), (order_in, order), (pairs_in, pairs), semaphores=small)
    device = lax.axis_index(AXIS)
    peer = peer_of(device)
    first = trig_table(angles, order, 0)
    second = trig_table(angles, order, 1)
    middle[0] = half_matrix(first, HIGH[:7])
    middle[1] = half_matrix(second, HIGH[:7], backwards=True)
    last[...] = row_matrix(second, range(7, 15))
    lanes[...] = lane_matrix(second, range(7))
    trig_out[0], trig_out[1] = first
    trig_out[2], trig_out[3] = second
    middle_bits = minus_bits(
        pairs, 0, 0, lambda block, row: high_bits(row) | peer << 10 | block << 7
    )
    last_bits = minus_bits(
        pairs, 1, BLOCKS, lambda block, row: row + BLOCK * block << 7 | device << 18
    )
    minus[...] = middle_bits | last_bits


def first_kernel(angles_in, order_in, state, out, angles, order, held, scratch, ready, small, arrived, sent):
    copies = []
    for pair in range(BLOCKS // 2):
        blocks = pl.ds(2 * pair, 2)
        copies.append(pltpu.make_async_copy(state.at[blocks], held.at[blocks], arrived.at[pair]))
        copies[-1].start()
    fetch((angles_in, angles), (order_in, order), semaphores=small)
    trig = trig_table(angles, order, 0)
    lanes = lane_matrix(trig, range(7))
    matrix = row_matrix(trig, range(7, 15))
    for copy in copies:
        copy.wait()
    rotate(held, slice_of, trig, matrix, lanes, None, out, scratch, ready, sent)


def slice_of(state, block, start):
    return state[block, pl.ds(start, SLICE), :]


def slice_backwards(state, block, start):
    chunk = (BLOCK * block + start) // 8
    return jnp.concatenate([state[255 - chunk - part] for part in range(SLICE // 8)], axis=0)


def rotate(state, load, trig, matrix, lanes, minus, out, scratch, ready, sent):
    for start in range(0, BLOCK, SLICE):
        rows = pl.ds(start, SLICE)
        parts = [load(state, block, start) for block in range(BLOCKS)]
        for block, part in enumerate(butterflies(parts, trig, range(15, 18))):
            scratch[block, rows, :] = part
    turned = [on_lanes(scratch[block], lanes) for block in range(BLOCKS)]
    copies = []
    size = BLOCKS // PARTS
    for part in range(PARTS):
        for here in range(size * part, size * (part + 1), 2):
            for block, values in enumerate(on_rows(matrix, turned[here], turned[here + 1]), here):
                ready[block] = values if minus is None else signed(values, minus, BLOCKS + block)
        blocks = pl.ds(size * part, size)
        copies.append(pltpu.make_async_copy(ready.at[blocks], out.at[blocks], sent.at[part]))
        copies[-1].start()
    for copy in copies:
        copy.wait()


def half_matrix(trig, qubits, backwards=False):
    high, low = split(kron_matrix(trig, qubits, backwards=backwards))
    return jnp.concatenate(
        [jnp.concatenate([high, high], axis=1), jnp.concatenate([low, jnp.zeros_like(low)], axis=1)],
        axis=0,
    )


def on_half(matrix, values):
    parts = jnp.concatenate(split(values), axis=0)
    both = jnp.dot(matrix, parts, preferred_element_type=jnp.float32)
    return both[:128] + both[128:]


def second_kernel(minus, matrices, trig, state, out):
    first, second = (trig[0], trig[1]), (trig[2], trig[3])
    sides = range(2)

    def rows(row, half):
        return pl.ds(row + 8 * 128 * half, 128, stride=8)

    turned = []
    for here in range(0, 8, 2):
        halves = []
        for half in sides:
            both = jnp.concatenate([state[rows(here + side, half), :] for side in sides], axis=1)
            halves.append(on_half(matrices[0], both))
        halves = butterflies(halves, first, HIGH[7:])
        for half in sides:
            bits = minus[pl.ds(128 * half, 128), :]
            both = halves[half][:, :128], halves[half][:, 128:]
            both = [signed(values, bits, here + side) for side, values in enumerate(both)]
            halves[half] = jnp.concatenate(both, axis=1)
        turned.append(butterflies(halves, second, HIGH[7:]))
    for here in range(0, 8, 2):
        for half in sides:
            both = on_half(matrices[1], turned[here // 2][half])
            out[rows(here, 1 - half), :], out[rows(here + 1, 1 - half), :] = both[:, :128], both[:, 128:]


def third_kernel(minus, matrix, lanes, trig, state, out, scratch, ready, sent):
    trig = trig[2], trig[3]
    rotate(state, slice_backwards, trig, matrix[...], lanes[...], minus[...], out, scratch, ready, sent)


HELD = pltpu.VMEM((ROWS, 128), jnp.float32)
IN_BLOCKS = pltpu.VMEM((BLOCKS, BLOCK, 128), jnp.float32)
PARAMS = pltpu.CompilerParams(vmem_limit_bytes=12 * 2**20)
VMEM, SMEM, HBM = (pl.BlockSpec(memory_space=space) for space in (pltpu.VMEM, pltpu.SMEM, pltpu.HBM))


def in_hbm(array):
    return pltpu.with_memory_space_constraint(array, pltpu.HBM)


def make_tables(angles, order, pairs):
    return pl.pallas_call(
        tables_kernel,
        out_shape=(
            pltpu.VMEM((BLOCK, 128), jnp.int32),
            pltpu.VMEM((2, 256, 256), jnp.bfloat16),
            pltpu.VMEM((256, 512), jnp.bfloat16),
            pltpu.VMEM((128, 256), jnp.bfloat16),
            pltpu.VMEM((4, 8, 128), jnp.float32),
        ),
        in_specs=[HBM] * 3,
        out_specs=(VMEM,) * 5,
        scratch_shapes=[
            pltpu.SMEM(angles.shape, jnp.float32),
            pltpu.SMEM(order.shape, jnp.int32),
            pltpu.SMEM(pairs.shape, jnp.int32),
            pltpu.SemaphoreType.DMA((3,)),
        ],
        compiler_params=PARAMS,
    )(*(in_hbm(array) for array in (angles, order, pairs)))


def first(angles, order, state):
    state = state.reshape(IN_BLOCKS.shape)
    return pl.pallas_call(
        first_kernel,
        out_shape=pltpu.HBM(IN_BLOCKS.shape, jnp.float32),
        in_specs=[HBM] * 3,
        out_specs=HBM,
        scratch_shapes=[
            pltpu.SMEM(angles.shape, jnp.float32),
            pltpu.SMEM(order.shape, jnp.int32),
            IN_BLOCKS,
            IN_BLOCKS,
            IN_BLOCKS,
            pltpu.SemaphoreType.DMA((2,)),
            pltpu.SemaphoreType.DMA((BLOCKS // 2,)),
            pltpu.SemaphoreType.DMA((PARTS,)),
        ],
        compiler_params=PARAMS,
    )(*(in_hbm(array) for array in (angles, order, state))).reshape(ROWS, 128)


def second(minus, matrices, trig, state):
    return pl.pallas_call(
        second_kernel, out_shape=HELD, in_specs=[VMEM] * 4, out_specs=VMEM, compiler_params=PARAMS
    )(minus, matrices, trig, state)


def third(minus, matrix, lanes, trig, state):
    return pl.pallas_call(
        third_kernel,
        out_shape=jax.ShapeDtypeStruct(IN_BLOCKS.shape, jnp.float32),
        in_specs=[VMEM] * 5,
        out_specs=HBM,
        scratch_shapes=[IN_BLOCKS, IN_BLOCKS, pltpu.SemaphoreType.DMA((PARTS,))],
        compiler_params=PARAMS,
    )(minus, matrix, lanes, trig, state.reshape(256, 8, 128))


def exchange(state, peers):
    chunks = state.reshape(256, 8, 128)
    return lax.all_to_all(chunks, AXIS, 0, 0, axis_index_groups=[peers], tiled=True).reshape(ROWS, 128)


def local(state_slab, angles, qubit_order, entangler_pairs):
    minus, middle, last, lanes, trig = make_tables(
        angles, qubit_order, entangler_pairs.transpose(0, 2, 1)
    )
    state = first(angles, qubit_order, state_slab.reshape(ROWS, 128))
    state = exchange(state, PEERS)
    state = second(minus, middle, trig, state)
    state = exchange(state, PEERS[::-1])
    state = third(minus, last, lanes, trig, state)
    return state.reshape(state_slab.shape)


def solution(mesh):
    in_specs = (P(AXIS, None), P(), P(), P())
    mesh = Mesh(mesh.devices.reshape(-1), (AXIS,))
    return jax.shard_map(local, mesh=mesh, in_specs=in_specs, out_specs=P(AXIS, None), check_vma=False)
```
